32 devices in a mesh: remap: 8 (over z, y), rep: 4 (over x, core).
Axes of the slice: x: 2, y: 2, z: 4, core: 2. Of those that a mesh axis runs over, the one named last changes fastest.
Arguments:
- amplitudes: bfloat16 [64, 1200, 1200], P('remap', None, 'rep'), may hold values from -6 to 6
- integrals: bfloat16 [1200, 1200, 128], P('remap', 'rep'), may hold values from -0.01953125 to 0.01953125
- orbital_irreps: int32 [1200], replicated, may hold values from 0 to 7
- slab_index: int32 [1], replicated, may hold values from 0 to 63
Outputs:
- residual: float32 [64, 128], P('remap', 'rep')
The draws below stay inside these ranges and needn't reach their ends.
All inputs are finite; a program needn't handle non-finite values.
Results may differ from the reference program's by a relative error of at most 0.0003.
Values may be sent and summed in bfloat16 or wider, within the bound.
No kernel may reach another device: no remote copies, remote signals or barrier semaphores. Data moves between devices by JAX's collectives and lax.ppermute only.
A program may use at most 128 MiB of HBM per device.

```python
import jax
import jax.numpy as jnp
from jax import lax

VIRT = 1200
SLABS = 64
AB = 128
PAIRS = 64
N_REMAP = 8


def touch_ends(entries, stream_key, low, high):
    shape = entries.shape
    index_at = [jax.random.randint(jax.random.fold_in(stream_key, axis), (), 0, shape[axis]) for axis in range(len(shape))]
    entries = entries.at[tuple(index_at)].set(low)
    longest = shape.index(max(shape))
    index_at[longest] = (index_at[longest] + 1) % shape[longest]
    return entries.at[tuple(index_at)].set(high)


def with_spikes(result, stream_key, source, target, blocks, factor):
    def block_of(position):
        return (jnp.arange(result.shape[position]) // (result.shape[position] // blocks)).reshape((-1,) + (1,) * (result.ndim - 1 - position))

    near = jax.random.permutation(stream_key, blocks)[block_of(target)]
    other_side = (block_of(target) + blocks // 2) % blocks
    return jnp.where((block_of(source) == near) | (block_of(source) == other_side), factor * result, result)


def block_scale(own_key, dims, split, smallest, top_value):
    def one(position, blocks):
        steps = jax.random.uniform(jax.random.fold_in(jax.random.fold_in(own_key, 6), position), (blocks,), jnp.float32, smallest / len(split), top_value / len(split))
        return jnp.repeat(jnp.exp(steps), dims[position] // blocks).reshape((-1,) + (1,) * (len(dims) - position - 1))

    loudness = one(*split[0])
    for cut in split[1:]:
        loudness = loudness * one(*cut)
    return loudness


def bell_draw_with(own_key, dims, width, reach, shards, heavy, kind=jnp.bfloat16):
    values = width * jax.random.normal(own_key, dims, jnp.float32)
    if shards:
        values = values * block_scale(own_key, dims, shards, -0.22, 0.18)
    return jnp.clip(with_spikes(values, jax.random.fold_in(own_key, 3), *heavy), -reach, reach).astype(kind)


def setup_inputs(seed: int = 0) -> dict:
    key_of = jax.random.split(jax.random.key(seed), 5)
    return {
        "amplitudes": bell_draw_with(key_of[0], (PAIRS, VIRT, VIRT), 1.0, 6.0, ((0, 8), (2, 4)), (1, 0, 8, 2.0)),
        "integrals": bell_draw_with(key_of[1], (VIRT, VIRT, AB), (VIRT * VIRT // 8) ** -0.5, 0.01953125, ((0, 8), (1, 4)), (1, 2, 4, 2.0)),
        "orbital_irreps": touch_ends(jax.random.randint(key_of[2], (VIRT,), 0, 8), jax.random.fold_in(key_of[2], 1), 0, 7).astype(jnp.int32),
        "slab_index": jax.random.randint(key_of[3], (1,), 0, SLABS).astype(jnp.int32),
    }


def reference(amplitudes, integrals, orbital_irreps, slab_index):
    stride = VIRT * VIRT // SLABS
    pair_ab = slab_index[0] * stride + jnp.arange(AB, dtype=jnp.int32)
    first_ab = (pair_ab // VIRT).astype(jnp.int32)
    second_ab = (pair_ab % VIRT).astype(jnp.int32)
    sym_ab = jnp.bitwise_xor(orbital_irreps[first_ab], orbital_irreps[second_ab])
    block_rows = VIRT // N_REMAP
    pair_count = amplitudes.shape[0]

    def add_block(index, total):
        start = (index * block_rows).astype(jnp.int32)
        amp_block = lax.dynamic_slice_in_dim(amplitudes, start, block_rows, 1)
        int_block = lax.dynamic_slice_in_dim(integrals, start, block_rows, 0)
        irr_c = lax.dynamic_slice_in_dim(orbital_irreps, start, block_rows, 0)
        sym_cd = jnp.bitwise_xor(irr_c[:, None], orbital_irreps[None, :])
        allowed = sym_cd[:, :, None] == sym_ab[None, None, :]
        blocked = jnp.where(allowed, int_block, jnp.zeros((), jnp.bfloat16))
        product = jnp.dot(amp_block.reshape(pair_count, block_rows * VIRT),
                          blocked.reshape(block_rows * VIRT, AB),
                          preferred_element_type=jnp.float32)
        return total + product

    total = lax.fori_loop(0, N_REMAP, add_block, jnp.zeros((pair_count, AB), jnp.float32))
    return 0.5 * total
```

```python
import jax
import jax.numpy as jnp
from jax import lax
from jax.sharding import PartitionSpec as P

SLABS = 64


def irrep_of(indices, table):
    matches = indices[:, None] == jnp.arange(table.shape[0], dtype=jnp.int32)[None, :]
    return jnp.sum(jnp.where(matches, table[None, :], 0), axis=1)


def reduce_to_owners(partial_term):
    remap, rep = lax.axis_size("remap"), lax.axis_size("rep")
    rows, cols = partial_term.shape
    blocks = partial_term.reshape(remap, rows // remap, rep, cols // rep)
    blocks = blocks.transpose(0, 2, 1, 3).reshape(remap * rep, rows // remap, cols // rep)
    arrived = lax.all_to_all(blocks, ("remap", "rep"), split_axis=0, concat_axis=0, tiled=True)
    return jnp.sum(arrived, axis=0)


def body(amplitudes, integrals, orbital_irreps, slab_index):
    c_rows, d_cols, ab_cols = integrals.shape
    virtual = orbital_irreps.shape[0]
    c_first = lax.axis_index("remap") * c_rows
    d_first = lax.axis_index("rep") * d_cols
    irr_c = lax.dynamic_slice_in_dim(orbital_irreps, c_first, c_rows, 0)
    irr_d = lax.dynamic_slice_in_dim(orbital_irreps, d_first, d_cols, 0)
    stride = virtual * virtual // SLABS
    pair_ab = slab_index[0] * stride + jnp.arange(ab_cols, dtype=jnp.int32)
    sym_ab = jnp.bitwise_xor(
        irrep_of(pair_ab // virtual, orbital_irreps), irrep_of(pair_ab % virtual, orbital_irreps)
    )
    sym_cd = jnp.bitwise_xor(irr_c[:, None], irr_d[None, :])
    allowed = sym_cd[:, :, None] == sym_ab[None, None, :]
    blocked = jnp.where(allowed, integrals, jnp.zeros((), jnp.bfloat16)).reshape(
        c_rows * d_cols, ab_cols
    )
    arrived = lax.all_to_all(amplitudes, "remap", split_axis=1, concat_axis=0, tiled=True)
    flattened = arrived.reshape(arrived.shape[0], c_rows * d_cols)
    partial_term = jnp.dot(flattened, blocked, preferred_element_type=jnp.float32)
    return 0.5 * reduce_to_owners(partial_term)


def solution(mesh):
    in_specs = (P("remap", None, "rep"), P("remap", "rep", None), P(), P())
    out_specs = P("remap", "rep")
    return jax.shard_map(body, mesh=mesh, in_specs=in_specs, out_specs=out_specs, check_vma=False)
```

```python
import functools

import jax
import jax.numpy as jnp
import numpy as np
from jax import lax
from jax.experimental import pallas as pl
from jax.experimental.pallas import tpu as pltpu
from jax.sharding import PartitionSpec as P

SLABS = 64
IRREPS = 8
BINS = 10
LEFT = 9
VMEM_BYTES = 48 * 1024 * 1024
BYTES_A_US = 3_600_000


def irrep_of(indices, table):
    matches = indices[:, None] == jnp.arange(table.shape[0], dtype=jnp.int32)[None, :]
    return jnp.sum(jnp.where(matches, table[None, :], 0), axis=1)


def reduce_to_owners(partial_term):
    remap, rep = lax.axis_size("remap"), lax.axis_size("rep")
    rows, cols = partial_term.shape
    blocks = partial_term.reshape(remap, rows // remap, rep, cols // rep)
    blocks = blocks.transpose(0, 2, 1, 3).reshape(remap * rep, rows // remap, cols // rep)
    arrived = lax.all_to_all(blocks, ("remap", "rep"), split_axis=0, concat_axis=0, tiled=True)
    return jnp.sum(arrived, axis=0)


def first_plus_one(match):
    c_plus_one = jnp.arange(1, match.shape[1] + 1, dtype=jnp.int32)
    return jnp.sum(jnp.where(match, c_plus_one[None, :, None], 0), axis=1)


def takes(us):
    return pl.CostEstimate(flops=0, bytes_accessed=int(us * BYTES_A_US), transcendentals=0)


def whole(array):
    zeros = (0,) * array.ndim
    return pl.BlockSpec(array.shape, lambda *_: zeros)


def split_lanes(d_cols):
    main = d_cols // 128 * 128
    tail = d_cols - main
    pitch = -(-tail // 8) * 8
    return main, tail, pitch


def pack_kernel(c_at, irrep_at, code_ref, integrals, out_ref, rows, arrived):
    bins = out_ref.shape[0]
    code = code_ref[...]

    def fetch(i):
        return pltpu.make_async_copy(integrals.at[c_at[i]], rows.at[i], arrived.at[i])

    def start(i, carry):
        fetch(i).start()
        return carry

    def one(g, carry):
        total = jnp.zeros(code.shape, jnp.float32)
        for h in range(IRREPS):
            i = g * IRREPS + h
            fetch(i).wait()
            total = jnp.where(code == irrep_at[i], rows[i].astype(jnp.float32), total)
        out_ref[g, pl.ds(0, code.shape[0])] = total.astype(out_ref.dtype)
        return carry

    lax.fori_loop(0, bins * IRREPS, start, 0)
    lax.fori_loop(0, bins, one, 0)


def pack(integrals, code, slots):
    _, d_cols, ab = integrals.shape
    padded = -(-d_cols // 16) * 16
    count = slots.shape[0]
    irrep = jnp.arange(count, dtype=jnp.int32) % IRREPS
    c_at = jnp.maximum(slots - 1, 0)
    irrep_at = jnp.where(slots > 0, irrep, IRREPS)
    out = jax.ShapeDtypeStruct((count // IRREPS, padded, ab), integrals.dtype)
    return pl.pallas_call(
        pack_kernel,
        out_shape=out,
        grid_spec=pltpu.PrefetchScalarGridSpec(
            num_scalar_prefetch=2,
            grid=(1,),
            in_specs=[whole(code), pl.BlockSpec(memory_space=pl.ANY)],
            out_specs=whole(out),
            scratch_shapes=[
                pltpu.VMEM((count, d_cols, ab), integrals.dtype),
                pltpu.SemaphoreType.DMA((count,)),
            ],
        ),
        cost_estimate=takes(4),
        compiler_params=pltpu.CompilerParams(vmem_limit_bytes=VMEM_BYTES),
        name="pack_bins",
    )(c_at, irrep_at, code, integrals)


def route_kernel(firsts, width, c_at, blocks, rows_ref, *outs):
    base = blocks[pl.program_id(0)] * width
    pair_rows, d_cols = rows_ref.shape[1:]
    main, tail, pitch = split_lanes(d_cols)
    for first, out in zip(firsts, outs):

        def one(group, carry):
            tails = []
            for i in range(IRREPS):
                at = c_at[base + (first + group) * IRREPS + i]
                out[0, group, :, pl.ds(i * main, main)] = rows_ref[at, :, pl.ds(0, main)]
                end = rows_ref[at, :, pl.ds(main, tail)].astype(jnp.float32)
                tails += [end, jnp.zeros((pair_rows, pitch - tail), jnp.float32)]
            ends = jnp.concatenate([x for x in tails if x.shape[1]], axis=1)
            out[0, group, :, pl.ds(IRREPS * main, IRREPS * pitch)] = ends.astype(out.dtype)
            return carry

        lax.fori_loop(0, out.shape[1], one, 0)


def route(by_c, c_at, blocks, spans, c_rows, by_block):
    pair_rows, d_cols = by_c.shape[1:]
    steps = blocks.shape[0]
    main, _, pitch = split_lanes(d_cols)
    lanes = IRREPS * (main + pitch)
    at_block = lambda i, c_at, blocks: (blocks[i], 0, 0, 0)
    in_order = lambda i, c_at, blocks: (i, 0, 0, 0)
    return pl.pallas_call(
        functools.partial(route_kernel, [first for first, _ in spans], c_at.shape[1]),
        out_shape=[
            jax.ShapeDtypeStruct((steps, groups, pair_rows, lanes), by_c.dtype)
            for _, groups in spans
        ],
        grid_spec=pltpu.PrefetchScalarGridSpec(
            num_scalar_prefetch=2,
            grid=(steps,),
            in_specs=[
                pl.BlockSpec(
                    (c_rows, pair_rows, d_cols), lambda i, c_at, blocks: (blocks[i], 0, 0)
                )
            ],
            out_specs=[
                pl.BlockSpec((1, groups, pair_rows, lanes), at_block if by_block else in_order)
                for _, groups in spans
            ],
        ),
        cost_estimate=takes(0.1 * steps * sum(groups for _, groups in spans)),
        compiler_params=pltpu.CompilerParams(vmem_limit_bytes=VMEM_BYTES),
        name="route_rows",
    )(c_at.reshape(-1), blocks, by_c)


def add_bins(total, bins, own, other, level, other_level, irr_d):
    pair_rows, d_cols = irr_d.shape
    main, tail, pitch = split_lanes(d_cols)

    def one(g, carry):
        def choose(lo, size, at):
            sides = [
                [
                    side[index, g, :, pl.ds(at(h), size)].astype(jnp.float32)
                    for h in range(IRREPS)
                ]
                for side, index in ((own, level), (other, other_level))
            ]
            irr = irr_d[:, lo : lo + size]
            rows = []
            for s in range(IRREPS):
                for side in sides:
                    value = side[s]
                    for j in range(1, IRREPS):
                        value = jnp.where(irr == j, side[s ^ j], value)
                    rows.append(value)
            lhs = jnp.concatenate(rows, axis=0).astype(bins.dtype)
            return jnp.dot(lhs, bins[g, pl.ds(lo, size)], preferred_element_type=jnp.float32)

        sum_ = choose(0, main, lambda h: h * main)
        if tail:
            sum_ += choose(main, tail, lambda h: IRREPS * main + h * pitch)
        total[...] += sum_
        return carry

    lax.fori_loop(0, bins.shape[0], one, 0)


def bins_kernel(places, info, irr_ref, sym_ref, own, near, far, *refs):
    half = near.shape[0]
    bins, (out, total) = refs[:-2], refs[-2:]
    irr_d, sym = irr_ref[...], sym_ref[...]
    total[...] = jnp.zeros_like(total)
    for place, part in zip(places, bins):

        @pl.when((info[place] >= 0) & (info[place] < half))
        def _():
            add_bins(total, part, own, near, info[place], info[place], irr_d)

        @pl.when(info[place] >= half)
        def _():
            add_bins(total, part, own, far, info[place], info[place] - half, irr_d)

    rows = out.shape[0]
    picked = jnp.zeros(out.shape, jnp.float32)
    for s in range(IRREPS):
        picked = jnp.where(sym == s, total[pl.ds(s * rows, rows), :], picked)
    out[...] = picked


def bins_product(places, parts, own, other, info, irr_d, sym):
    pair_rows, ab = irr_d.shape[0], sym.shape[1]
    out = jax.ShapeDtypeStruct((2 * pair_rows, ab), jnp.float32)
    tensors = [irr_d, sym, own, *other, *parts]
    return pl.pallas_call(
        functools.partial(bins_kernel, places),
        out_shape=out,
        grid_spec=pltpu.PrefetchScalarGridSpec(
            num_scalar_prefetch=1,
            grid=(1,),
            in_specs=[whole(x) for x in tensors],
            out_specs=whole(out),
            scratch_shapes=[pltpu.VMEM((IRREPS * 2 * pair_rows, ab), jnp.float32)],
        ),
        cost_estimate=takes(3),
        compiler_params=pltpu.CompilerParams(vmem_limit_bytes=VMEM_BYTES),
        name="bins_product",
    )(info, *tensors)


def left_kernel(c_at, irrep_at, code_ref, amp_ref, integrals, out_ref, rows, arrived):
    sources, groups, pair_rows, _ = amp_ref.shape
    d_cols, ab = code_ref.shape
    main, tail, pitch = split_lanes(d_cols)

    def fetch(i):
        return pltpu.make_async_copy(integrals.at[c_at[i]], rows.at[i], arrived.at[i])

    def start(i, carry):
        fetch(i).start()
        return carry

    lax.fori_loop(0, groups * IRREPS, start, 0)
    out_ref[...] = jnp.zeros_like(out_ref)

    def one(group, carry):
        amps = amp_ref[:, group].astype(jnp.float32)
        amps = amps.reshape(sources * pair_rows, amps.shape[2]).astype(rows.dtype)
        total = jnp.zeros(out_ref.shape, jnp.float32)
        ends = []
        for h in range(IRREPS):
            i = group * IRREPS + h
            fetch(i).wait()
            row = jnp.where(code_ref[...] == irrep_at[i], rows[i].astype(jnp.float32), 0.0)
            total += jnp.dot(
                amps[:, h * main : (h + 1) * main], row[:main].astype(rows.dtype),
                preferred_element_type=jnp.float32,
            )
            ends += [row[main:], jnp.zeros((pitch - tail, ab), jnp.float32)]
        if tail:
            total += jnp.dot(
                amps[:, IRREPS * main :],
                jnp.concatenate([x for x in ends if x.shape[0]], axis=0).astype(rows.dtype),
                preferred_element_type=jnp.float32,
            )
        out_ref[...] += total
        return carry

    lax.fori_loop(0, groups, one, 0)


def left_product(amps, integrals, code, slots, irreps):
    sources, groups, pair_rows, _ = amps.shape
    d_cols, ab = code.shape
    count = groups * IRREPS
    c_at = jnp.maximum(slots - 1, 0)
    irrep_at = jnp.where(slots > 0, irreps, IRREPS)
    out = jax.ShapeDtypeStruct((sources * pair_rows, ab), jnp.float32)
    return pl.pallas_call(
        left_kernel,
        out_shape=out,
        grid_spec=pltpu.PrefetchScalarGridSpec(
            num_scalar_prefetch=2,
            grid=(1,),
            in_specs=[whole(code), whole(amps), pl.BlockSpec(memory_space=pl.ANY)],
            out_specs=whole(out),
            scratch_shapes=[
                pltpu.VMEM((count, d_cols, ab), integrals.dtype),
                pltpu.SemaphoreType.DMA((count,)),
            ],
        ),
        cost_estimate=takes(1.5 * groups),
        compiler_params=pltpu.CompilerParams(vmem_limit_bytes=VMEM_BYTES),
        name="left_product",
    )(c_at, irrep_at, code, amps, integrals)


def body(amplitudes, integrals, orbital_irreps, slab_index):
    c_rows, d_cols, ab_cols = integrals.shape
    pair_rows = amplitudes.shape[0]
    virtual = orbital_irreps.shape[0]
    blocks = lax.axis_size("remap")
    sides = 2
    levels = blocks // sides
    assert levels >= 2 and blocks == levels * sides
    block = lax.axis_index("remap")
    level, side = block // sides, block % sides
    left = LEFT * IRREPS

    irr_blocks = orbital_irreps.reshape(blocks, c_rows)
    earlier = jnp.arange(c_rows)[:, None] < jnp.arange(c_rows)[None, :]
    alike = (irr_blocks[:, :, None] == irr_blocks[:, None, :]) & earlier[None]
    rank = jnp.sum(alike.astype(jnp.int32), axis=1)
    over = rank >= BINS
    left_rank = jnp.sum((over[:, :, None] & earlier[None]).astype(jnp.int32), axis=1)
    left_rounds = (jnp.max(jnp.sum(over.astype(jnp.int32), axis=1)) + left - 1) // left
    key = jnp.where(over, BINS * IRREPS + left_rank, rank * IRREPS + irr_blocks)

    def table(first, count):
        wanted = first + jnp.arange(count, dtype=jnp.int32)
        return first_plus_one(key[:, :, None] == wanted[None, None, :])

    slots = table(0, BINS * IRREPS + left)
    own_slots = lax.dynamic_index_in_dim(slots, block, 0, False)
    own_irr = lax.dynamic_index_in_dim(irr_blocks, block, 0, False)

    irr_d = lax.dynamic_slice_in_dim(orbital_irreps, lax.axis_index("rep") * d_cols, d_cols, 0)
    stride = virtual * virtual // SLABS
    pair_ab = slab_index[0] * stride + jnp.arange(ab_cols, dtype=jnp.int32)
    sym_ab = jnp.bitwise_xor(
        irrep_of(pair_ab // virtual, orbital_irreps), irrep_of(pair_ab % virtual, orbital_irreps)
    )
    code = jnp.bitwise_xor(irr_d[:, None], sym_ab[None, :])
    irr_rows = jnp.broadcast_to(irr_d[None, :], (pair_rows, d_cols))

    order = [1, 0] + list(range(2, levels))

    def at_level(z, a):
        return a if z < levels // 2 else levels - 1 - a

    plan = []
    for z in range(levels):
        for b in range(sides):
            row = [at_level(z, a) * sides + c for c in (1 - b, b) for a in order]
            for t in range(levels):
                for a in (z - t, z + t):
                    row.append(order.index(at_level(z, a)) if 0 <= a < levels else -1)
            plan.append(row)
    info = lax.dynamic_index_in_dim(jnp.asarray(np.array(plan, np.int32)), block, 0, False)

    bins = pack(integrals, code, own_slots[: BINS * IRREPS])
    amplitudes, bins = lax.optimization_barrier((amplitudes, bins))
    by_c = amplitudes.transpose(1, 0, 2)

    def hops(pairs, swap):
        return [
            (a * sides + b, c * sides + (sides - 1 - b if swap else b))
            for a, c in pairs
            for b in range(sides)
        ]

    rounds = [(bins, bins)]
    for t in range(1, levels):
        up = [(z, z + 1) for z in range(t - 1, levels - 1)]
        down = [(levels - 1 - a, levels - 1 - c) for a, c in up]
        rounds.append(
            (
                lax.ppermute(rounds[-1][0], "remap", hops(up, False)),
                lax.ppermute(rounds[-1][1], "remap", hops(down, False)),
            )
        )
    c_at = jnp.maximum(slots - 1, 0)
    in_bins = [(0, BINS)]
    cuts = [(0, LEFT)]
    half = levels // 2
    stay = hops([(z, z) for z in range(levels)], True)
    other = []
    for lo, hi in ((0, half), (half, levels)):
        (cross,) = route(by_c, c_at, info[lo:hi], in_bins, c_rows, False)
        other.append(lax.ppermute(cross, "remap", stay))
    by_c, rounds[1] = lax.optimization_barrier((by_c, rounds[1]))
    (own,) = route(by_c, c_at, info[levels:blocks], in_bins, c_rows, False)
    every = jnp.arange(blocks, dtype=jnp.int32)
    sent = route(
        by_c, c_at, every, [(BINS + first, groups) for first, groups in cuts], c_rows, True
    )
    sent = list(sent)
    sent, rounds[2], other[0] = lax.optimization_barrier((sent, rounds[2], other[0]))
    mine = 0
    for t, parts in enumerate(rounds):
        places = [blocks + 2 * t, blocks + 2 * t + 1]
        if t == 0:
            places, parts = places[:1], parts[:1]
        mine += bins_product(places, parts, own, other, info, irr_rows, sym_ab[None, :])

    def left_term(sent, left_slots):
        arrived = lax.all_to_all(sent, "remap", split_axis=0, concat_axis=0, tiled=True)
        mine = lax.dynamic_index_in_dim(left_slots, block, 0, False)
        at = jnp.arange(1, c_rows + 1, dtype=jnp.int32)
        irreps = jnp.sum(jnp.where(mine[:, None] == at[None, :], own_irr[None, :], 0), axis=1)
        return left_product(arrived, integrals, code, mine, irreps)

    def next_round(index, total):
        left_slots = table(BINS * IRREPS + index * left, left)
        (sent,) = route(
            by_c, jnp.maximum(left_slots - 1, 0), every, [(0, LEFT)], c_rows, True
        )
        return total + left_term(sent, left_slots)

    total = 0
    for (first, _), part in zip(cuts, sent):
        lo = (BINS + first) * IRREPS
        total += left_term(part, slots[:, lo : lo + part.shape[1] * IRREPS])
    total = lax.fori_loop(1, left_rounds, next_round, total)

    total = total.reshape(blocks, pair_rows, ab_cols)
    ids = jnp.arange(blocks)[:, None, None]
    total = total + jnp.where(ids == block, mine[None, :pair_rows], 0.0)
    total = total + jnp.where(ids == level * sides + 1 - side, mine[None, pair_rows:], 0.0)
    return 0.5 * reduce_to_owners(total.reshape(blocks * pair_rows, ab_cols))


def solution(mesh):
    in_specs = (P("remap", None, "rep"), P("remap", "rep", None), P(), P())
    out_specs = P("remap", "rep")
    return jax.shard_map(body, mesh=mesh, in_specs=in_specs, out_specs=out_specs, check_vma=False)
```

```python
import functools

import jax
import jax.numpy as jnp
import numpy as np
from jax import lax
from jax.experimental import pallas as pl
from jax.experimental.pallas import tpu as pltpu
from jax.sharding import PartitionSpec as P

SLABS = 64
IRREPS = 8
BINS = 10
LEFT = 9
VMEM_BYTES = 48 * 1024 * 1024
BYTES_A_US = 3_600_000


def irrep_of(indices, table):
    matches = indices[:, None] == jnp.arange(table.shape[0], dtype=jnp.int32)[None, :]
    return jnp.sum(jnp.where(matches, table[None, :], 0), axis=1)


def sum_kernel(parts_ref, out_ref):
    rows, cols = out_ref.shape
    total = jnp.sum(parts_ref[...], axis=0)
    out_ref[...] = jnp.concatenate(
        [total[:, r * cols : (r + 1) * cols] for r in range(rows)], axis=0
    )


def reduce_to_owners(partial_term):
    remap, rep = lax.axis_size("remap"), lax.axis_size("rep")
    rows, cols = partial_term.shape
    blocks = partial_term.reshape(remap, rows // remap, rep, cols // rep)
    blocks = blocks.transpose(0, 2, 1, 3).reshape(remap * rep, 1, -1)
    arrived = lax.all_to_all(blocks, ("remap", "rep"), split_axis=0, concat_axis=0, tiled=True)
    return pl.pallas_call(
        sum_kernel,
        out_shape=jax.ShapeDtypeStruct((rows // remap, cols // rep), jnp.float32),
        name="sum_parts",
    )(arrived)


def first_plus_one(match):
    c_plus_one = jnp.arange(1, match.shape[1] + 1, dtype=jnp.int32)
    return jnp.sum(jnp.where(match, c_plus_one[None, :, None], 0), axis=1)


def takes(us):
    return pl.CostEstimate(flops=0, bytes_accessed=int(us * BYTES_A_US), transcendentals=0)


def whole(array):
    zeros = (0,) * array.ndim
    return pl.BlockSpec(array.shape, lambda *_: zeros)


def split_lanes(d_cols):
    main = d_cols // 128 * 128
    tail = d_cols - main
    pitch = -(-tail // 16) * 16
    return main, tail, pitch


def pack_kernel(irreps, slab, integrals, out_ref, rows, code_ref, counts, arrived):
    c_rows, d_cols, ab = integrals.shape
    bins = out_ref.shape[0]
    virtual = irreps.shape[0]

    def fetch(c, i):
        return pltpu.make_async_copy(integrals.at[c], rows.at[i], arrived.at[i])

    for h in range(IRREPS):
        counts[h] = 0
    c_first = lax.axis_index("remap") * c_rows

    def place(c, carry):
        h = irreps[c_first + c]
        g = counts[h]
        counts[h] = g + 1

        @pl.when(g < bins)
        def _():
            fetch(c, g * IRREPS + h).start()

        return carry

    lax.fori_loop(0, c_rows, place, 0, unroll=15)

    pair = slab[0] * (virtual * virtual // SLABS)
    a_first = pair // virtual
    b_first = pair - a_first * virtual
    lane = lax.broadcasted_iota(jnp.int32, (1, ab), 1)

    def symmetry(k, sym):
        over = (b_first + k >= virtual).astype(jnp.int32)
        value = irreps[a_first + over] ^ irreps[b_first + k - over * virtual]
        return jnp.where(lane == k, value, sym)

    sym = lax.fori_loop(0, ab, symmetry, jnp.zeros((1, ab), jnp.int32), unroll=32)
    d_first = lax.axis_index("rep") * d_cols

    def code_row(d, carry):
        code_ref[pl.ds(d, 1), :] = sym ^ irreps[d_first + d]
        return carry

    lax.fori_loop(0, d_cols, code_row, 0, unroll=50)

    code = code_ref[...].astype(jnp.float32).astype(rows.dtype)

    def one(g, carry):
        for h in range(IRREPS):
            i = g * IRREPS + h

            @pl.when(g < counts[h])
            def _():
                fetch(0, i).wait()

            @pl.when(g >= counts[h])
            def _():
                rows[i] = jnp.zeros((d_cols, ab), rows.dtype)

        total = rows[g * IRREPS]
        for h in range(1, IRREPS):
            total = jnp.where(code == h, rows[g * IRREPS + h], total)
        out_ref[g, pl.ds(0, d_cols)] = total
        return carry

    lax.fori_loop(0, bins, one, 0)


def pack(integrals, irreps, slab):
    _, d_cols, ab = integrals.shape
    padded = -(-d_cols // 16) * 16
    out = jax.ShapeDtypeStruct((BINS, padded, ab), integrals.dtype)
    return pl.pallas_call(
        pack_kernel,
        out_shape=out,
        grid_spec=pltpu.PrefetchScalarGridSpec(
            num_scalar_prefetch=2,
            grid=(1,),
            in_specs=[pl.BlockSpec(memory_space=pl.ANY)],
            out_specs=whole(out),
            scratch_shapes=[
                pltpu.VMEM((BINS * IRREPS, d_cols, ab), integrals.dtype),
                pltpu.VMEM((d_cols, ab), jnp.int32),
                pltpu.SMEM((IRREPS,), jnp.int32),
                pltpu.SemaphoreType.DMA((BINS * IRREPS,)),
            ],
        ),
        cost_estimate=takes(4),
        compiler_params=pltpu.CompilerParams(vmem_limit_bytes=VMEM_BYTES),
        name="pack_bins",
    )(irreps, slab, integrals)


def route_kernel(firsts, width, c_at, blocks, rows_ref, *outs):
    base = blocks[pl.program_id(0)] * width
    pair_rows, d_cols = rows_ref.shape[1:]
    main, tail, pitch = split_lanes(d_cols)
    for first, out in zip(firsts, outs):

        def one(group, carry):
            tails = []
            for i in range(IRREPS):
                at = c_at[base + (first + group) * IRREPS + i]
                out[0, group, :, pl.ds(i * main, main)] = rows_ref[at, :, pl.ds(0, main)]
                end = rows_ref[at, :, pl.ds(main, tail)].astype(jnp.float32)
                tails += [end, jnp.zeros((pair_rows, pitch - tail), jnp.float32)]
            ends = jnp.concatenate([x for x in tails if x.shape[1]], axis=1)
            out[0, group, :, pl.ds(IRREPS * main, IRREPS * pitch)] = ends.astype(out.dtype)
            return carry

        lax.fori_loop(0, out.shape[1], one, 0)


def route(by_c, c_at, blocks, spans, c_rows, by_block):
    pair_rows, d_cols = by_c.shape[1:]
    steps = blocks.shape[0]
    main, _, pitch = split_lanes(d_cols)
    lanes = IRREPS * (main + pitch)
    at_block = lambda i, c_at, blocks: (blocks[i], 0, 0, 0)
    in_order = lambda i, c_at, blocks: (i, 0, 0, 0)
    return pl.pallas_call(
        functools.partial(route_kernel, [first for first, _ in spans], c_at.shape[1]),
        out_shape=[
            jax.ShapeDtypeStruct((steps, groups, pair_rows, lanes), by_c.dtype)
            for _, groups in spans
        ],
        grid_spec=pltpu.PrefetchScalarGridSpec(
            num_scalar_prefetch=2,
            grid=(steps,),
            in_specs=[
                pl.BlockSpec(
                    (c_rows, pair_rows, d_cols), lambda i, c_at, blocks: (blocks[i], 0, 0)
                )
            ],
            out_specs=[
                pl.BlockSpec((1, groups, pair_rows, lanes), at_block if by_block else in_order)
                for _, groups in spans
            ],
        ),
        cost_estimate=takes(0.1 * steps * sum(groups for _, groups in spans)),
        compiler_params=pltpu.CompilerParams(vmem_limit_bytes=VMEM_BYTES),
        name="route_rows",
    )(c_at.reshape(-1), blocks, by_c)


def chosen_rows(g, lo, size, own, other, level, other_level, irr_d, dtype):
    main, _, pitch = split_lanes(irr_d.shape[1])

    def lane(h):
        return h * main if lo < main else IRREPS * main + h * pitch

    sides = [
        [side[at, g, :, pl.ds(lane(h), size)].astype(jnp.float32) for h in range(IRREPS)]
        for side, at in ((own, level), (other, other_level))
    ]
    irr = irr_d[:, lo : lo + size]
    rows = []
    for s in range(IRREPS):
        for side in sides:
            value = side[s]
            for j in range(1, IRREPS):
                value = jnp.where(irr == j, side[s ^ j], value)
            rows.append(value)
    return jnp.concatenate(rows, axis=0).astype(dtype)


def spans_of(d_cols):
    main, tail, _ = split_lanes(d_cols)
    return [(0, main), (main, tail)] if tail else [(0, main)]


def add_bins(total, bins, own, other, level, other_level, irr_d):
    def one(g, carry):
        sum_ = total[...]
        for lo, size in spans_of(irr_d.shape[1]):
            lhs = chosen_rows(g, lo, size, own, other, level, other_level, irr_d, bins.dtype)
            sum_ += jnp.dot(lhs, bins[g, pl.ds(lo, size)], preferred_element_type=jnp.float32)
        total[...] = sum_
        return carry

    lax.fori_loop(0, bins.shape[0], one, 0)


def pick_symmetry(total, sym, rows):
    picked = jnp.zeros((rows, total.shape[1]), jnp.float32)
    for s in range(IRREPS):
        picked = jnp.where(sym == s, total[pl.ds(s * rows, rows), :], picked)
    return picked


def choose_kernel(places, n_other, info, irr_ref, own, *refs):
    others, out = refs[:n_other], refs[n_other]
    irr_d = irr_ref[...]
    level, first = jnp.maximum(info[places[0]], info[places[1]]), 0
    for other in others:
        last = first + other.shape[0]

        @pl.when((level >= first) & (level < last))
        def _():
            def one(g, carry):
                for lo, size in spans_of(irr_d.shape[1]):
                    out[g, :, pl.ds(lo, size)] = chosen_rows(
                        g, lo, size, own, other, level, level - first, irr_d, out.dtype
                    )
                return carry

            lax.fori_loop(0, out.shape[0], one, 0)

        first = last


def choose(places, own, other, info, irr_d):
    pair_rows, d_cols = irr_d.shape
    tensors = [irr_d, own, *other]
    return pl.pallas_call(
        functools.partial(choose_kernel, places, len(other)),
        out_shape=jax.ShapeDtypeStruct((BINS, IRREPS * 2 * pair_rows, d_cols), own.dtype),
        grid_spec=pltpu.PrefetchScalarGridSpec(
            num_scalar_prefetch=1,
            grid=(1,),
            in_specs=[pl.BlockSpec(memory_space=pltpu.VMEM)] * len(tensors),
            out_specs=pl.BlockSpec(memory_space=pltpu.VMEM),
        ),
        cost_estimate=takes(3),
        compiler_params=pltpu.CompilerParams(vmem_limit_bytes=VMEM_BYTES // 3),
        name="choose_rows",
    )(info, *tensors)


def last_kernel(places, info, sym_ref, chosen, *refs):
    bins, (out, total) = refs[:2], refs[2:]
    total[...] = jnp.zeros_like(total)
    for place, part in zip(places, bins):

        @pl.when(info[place] >= 0)
        def _():
            sum_ = jnp.zeros(total.shape, jnp.float32)
            for g in range(part.shape[0]):
                sum_ += jnp.dot(
                    chosen[g], part[g, pl.ds(0, chosen.shape[2])],
                    preferred_element_type=jnp.float32,
                )
            total[...] = sum_

    out[...] = pick_symmetry(total, sym_ref[...], out.shape[0])


def last_product(places, parts, chosen, info, sym):
    rows, ab = chosen.shape[1], sym.shape[1]
    out = jax.ShapeDtypeStruct((rows // IRREPS, ab), jnp.float32)
    tensors = [sym, chosen, *parts]
    return pl.pallas_call(
        functools.partial(last_kernel, places),
        out_shape=out,
        grid_spec=pltpu.PrefetchScalarGridSpec(
            num_scalar_prefetch=1,
            grid=(1,),
            in_specs=[pl.BlockSpec(memory_space=pltpu.VMEM)] * len(tensors),
            out_specs=whole(out),
            scratch_shapes=[pltpu.VMEM((rows, ab), jnp.float32)],
        ),
        cost_estimate=takes(2),
        compiler_params=pltpu.CompilerParams(vmem_limit_bytes=VMEM_BYTES // 3),
        name="last_product",
    )(info, *tensors)


def bins_kernel(places, n_other, info, irr_ref, sym_ref, own, *refs):
    others, refs = refs[:n_other], refs[n_other:]
    bins, (out, total) = refs[:-2], refs[-2:]
    irr_d, sym = irr_ref[...], sym_ref[...]
    total[...] = jnp.zeros_like(total)
    for place, part in zip(places, bins):
        level, first = info[place], 0
        for other in others:
            last = first + other.shape[0]

            @pl.when((level >= first) & (level < last))
            def _():
                add_bins(total, part, own, other, level, level - first, irr_d)

            first = last

    out[...] = pick_symmetry(total, sym, out.shape[0])


def bins_product(places, parts, own, other, info, irr_d, sym):
    pair_rows, ab = irr_d.shape[0], sym.shape[1]
    out = jax.ShapeDtypeStruct((2 * pair_rows, ab), jnp.float32)
    tensors = [irr_d, sym, own, *other, *parts]
    return pl.pallas_call(
        functools.partial(bins_kernel, places, len(other)),
        out_shape=out,
        grid_spec=pltpu.PrefetchScalarGridSpec(
            num_scalar_prefetch=1,
            grid=(1,),
            in_specs=[pl.BlockSpec(memory_space=pltpu.VMEM)] * len(tensors),
            out_specs=whole(out),
            scratch_shapes=[pltpu.VMEM((IRREPS * 2 * pair_rows, ab), jnp.float32)],
        ),
        cost_estimate=takes(3),
        compiler_params=pltpu.CompilerParams(vmem_limit_bytes=VMEM_BYTES // 3),
        name="bins_product",
    )(info, *tensors)


def left_rows_kernel(slots, irreps, code_ref, integrals, out_ref, rows, arrived):
    group = pl.program_id(0)
    d_cols, ab = code_ref.shape
    main, tail, pitch = split_lanes(d_cols)

    def fetch(i):
        c = jnp.maximum(slots[i] - 1, 0)
        return pltpu.make_async_copy(integrals.at[c], rows.at[i], arrived.at[i])

    def start(i, carry):
        fetch(i).start()
        return carry

    @pl.when(group == 0)
    def _():
        lax.fori_loop(0, rows.shape[0], start, 0)

    code = code_ref[...]
    for h in range(IRREPS):
        i = group * IRREPS + h
        fetch(i).wait()
        irrep = jnp.where(slots[i] > 0, irreps[i], IRREPS)
        row = jnp.where(code == irrep, rows[i].astype(jnp.float32), 0.0)
        out_ref[0, pl.ds(h * main, main)] = row[:main].astype(out_ref.dtype)
        if tail:
            end = row[main:]
            if pitch > tail:
                end = jnp.concatenate([end, jnp.zeros((pitch - tail, ab), jnp.float32)], axis=0)
            out_ref[0, pl.ds(IRREPS * main + h * pitch, pitch)] = end.astype(out_ref.dtype)


def left_rows(integrals, code, slots, irreps):
    d_cols, ab = code.shape
    count = slots.shape[0]
    main, _, pitch = split_lanes(d_cols)
    depth = IRREPS * (main + pitch)
    return pl.pallas_call(
        left_rows_kernel,
        out_shape=jax.ShapeDtypeStruct((count // IRREPS, depth, ab), integrals.dtype),
        grid_spec=pltpu.PrefetchScalarGridSpec(
            num_scalar_prefetch=2,
            grid=(count // IRREPS,),
            in_specs=[whole(code), pl.BlockSpec(memory_space=pl.ANY)],
            out_specs=pl.BlockSpec((1, depth, ab), lambda i, *_: (i, 0, 0)),
            scratch_shapes=[
                pltpu.VMEM((count, d_cols, ab), integrals.dtype),
                pltpu.SemaphoreType.DMA((count,)),
            ],
        ),
        cost_estimate=takes(5),
        compiler_params=pltpu.CompilerParams(vmem_limit_bytes=VMEM_BYTES),
        name="left_rows",
    )(slots, irreps, code, integrals)


def left_kernel(amp_ref, row_ref, out_ref):
    sources, groups, pair_rows, depth = amp_ref.shape
    step = pl.program_id(0)

    @pl.when(step == 0)
    def _():
        out_ref[...] = jnp.zeros_like(out_ref)

    total = out_ref[...]
    for g in range(groups):
        amps = amp_ref[:, g].astype(jnp.float32).reshape(sources * pair_rows, depth)
        total += jnp.dot(
            amps.astype(row_ref.dtype), row_ref[step * groups + g],
            preferred_element_type=jnp.float32,
        )
    out_ref[...] = total


def left_product(amps, rows):
    sources, groups, pair_rows, depth = amps.shape
    ab = rows.shape[2]
    at_once = max(n for n in (1, 2, 3) if groups % n == 0)
    return pl.pallas_call(
        left_kernel,
        out_shape=jax.ShapeDtypeStruct((sources * pair_rows, ab), jnp.float32),
        grid=(groups // at_once,),
        in_specs=[
            pl.BlockSpec((sources, at_once, pair_rows, depth), lambda i: (0, i, 0, 0)),
            pl.BlockSpec(memory_space=pltpu.VMEM),
        ],
        out_specs=pl.BlockSpec((sources * pair_rows, ab), lambda i: (0, 0)),
        cost_estimate=takes(5),
        compiler_params=pltpu.CompilerParams(vmem_limit_bytes=VMEM_BYTES),
        name="left_product",
    )(amps, rows)


def body(amplitudes, integrals, orbital_irreps, slab_index):
    c_rows, d_cols, ab_cols = integrals.shape
    pair_rows = amplitudes.shape[0]
    virtual = orbital_irreps.shape[0]
    blocks = lax.axis_size("remap")
    sides = 2
    levels = blocks // sides
    assert levels >= 2 and blocks == levels * sides
    block = lax.axis_index("remap")
    level, side = block // sides, block % sides
    left = LEFT * IRREPS

    bins = pack(integrals, orbital_irreps, slab_index)
    amplitudes, orbital_irreps, bins = lax.optimization_barrier((amplitudes, orbital_irreps, bins))

    earlier = jnp.arange(c_rows)[:, None] < jnp.arange(c_rows)[None, :]

    def places_of(irr):
        alike = (irr[:, :, None] == irr[:, None, :]) & earlier[None]
        rank = jnp.sum(alike.astype(jnp.int32), axis=1)
        over = rank >= BINS
        left_rank = jnp.sum((over[:, :, None] & earlier[None]).astype(jnp.int32), axis=1)
        return jnp.where(over, BINS * IRREPS + left_rank, rank * IRREPS + irr)

    def table(places, first, count):
        wanted = first + jnp.arange(count, dtype=jnp.int32)
        return first_plus_one(places[:, :, None] == wanted[None, None, :])

    own_irr = lax.dynamic_slice_in_dim(orbital_irreps, block * c_rows, c_rows, 0)
    own_places = places_of(own_irr[None])

    def own_left(index):
        first = BINS * IRREPS + index * left
        match = own_places[0][:, None] == first + jnp.arange(left, dtype=jnp.int32)[None, :]
        irreps = jnp.sum(jnp.where(match, own_irr[:, None], 0), axis=0)
        return first_plus_one(match[None])[0], irreps

    irr_d = lax.dynamic_slice_in_dim(orbital_irreps, lax.axis_index("rep") * d_cols, d_cols, 0)
    stride = virtual * virtual // SLABS
    pair_ab = slab_index[0] * stride + jnp.arange(ab_cols, dtype=jnp.int32)
    sym_ab = jnp.bitwise_xor(
        irrep_of(pair_ab // virtual, orbital_irreps), irrep_of(pair_ab % virtual, orbital_irreps)
    )
    code = jnp.bitwise_xor(irr_d[:, None], sym_ab[None, :])
    irr_rows = jnp.broadcast_to(irr_d[None, :], (pair_rows, d_cols))

    order = [1, 0] + list(range(2, levels))

    def at_level(z, a):
        return a if z < levels // 2 else levels - 1 - a

    plan = []
    for z in range(levels):
        for b in range(sides):
            row = [at_level(z, a) * sides + c for c in (1 - b, b) for a in order]
            for t in range(levels):
                for a in (z - t, z + t):
                    row.append(order.index(at_level(z, a)) if 0 <= a < levels else -1)
            plan.append(row)
    info = lax.dynamic_index_in_dim(jnp.asarray(np.array(plan, np.int32)), block, 0, False)

    by_c = amplitudes.transpose(1, 0, 2)

    def hops(pairs, swap):
        return [
            (a * sides + b, c * sides + (sides - 1 - b if swap else b))
            for a, c in pairs
            for b in range(sides)
        ]

    rounds = [(bins, bins)]
    for t in range(1, levels):
        up = [(z, z + 1) for z in range(t - 1, levels - 1)]
        down = [(levels - 1 - a, levels - 1 - c) for a, c in up]
        rounds.append(
            (
                lax.ppermute(rounds[-1][0], "remap", hops(up, False)),
                lax.ppermute(rounds[-1][1], "remap", hops(down, False)),
            )
        )
    places = places_of(orbital_irreps.reshape(blocks, c_rows))
    left_rounds = (jnp.max(places) - BINS * IRREPS + left) // left
    c_at = jnp.maximum(table(places, 0, BINS * IRREPS + left) - 1, 0)
    in_bins = [(0, BINS)]
    split = levels // 2
    stay = hops([(z, z) for z in range(levels)], True)
    def left_term(sent, rows):
        arrived = lax.all_to_all(sent, "remap", split_axis=0, concat_axis=0, tiled=True)
        return left_product(arrived, rows)

    (near,) = route(by_c, c_at, info[:split], in_bins, c_rows, False)
    near = lax.ppermute(near, "remap", stay)
    by_c, rounds[1] = lax.optimization_barrier((by_c, rounds[1]))
    every = jnp.arange(blocks, dtype=jnp.int32)
    (sent,) = route(by_c, c_at, every, [(BINS, LEFT)], c_rows, True)
    (far,) = route(by_c, c_at, info[split:levels], in_bins, c_rows, False)
    (own,) = route(by_c, c_at, info[levels:blocks], in_bins, c_rows, False)
    left_at = own_left(0)
    sent, far, own, left_at, near, rounds[2], code, irr_rows, sym_ab = lax.optimization_barrier(
        (sent, far, own, left_at, near, rounds[2], code, irr_rows, sym_ab)
    )
    other = [near, lax.ppermute(far, "remap", stay)]
    total = left_term(sent, left_rows(integrals, code, *left_at))
    rounds[-1], total = lax.optimization_barrier((rounds[-1], total))
    mine = 0
    for t, parts in enumerate(rounds):
        ways = [blocks + 2 * t, blocks + 2 * t + 1]
        if t == 0:
            ways, parts = ways[:1], parts[:1]
        reach = max(row[way] for row in plan for way in ways)
        if t == levels - 1:
            chosen = choose(ways, own, other, info, irr_rows)
            mine += last_product(ways, parts, chosen, info, sym_ab[None, :])
            continue
        mine += bins_product(ways, parts, own, other[: 1 + (reach >= split)], info, irr_rows, sym_ab[None, :])

    def next_round(index, total):
        c_at = jnp.maximum(table(places, BINS * IRREPS + index * left, left) - 1, 0)
        (sent,) = route(by_c, c_at, every, [(0, LEFT)], c_rows, True)
        return total + left_term(sent, left_rows(integrals, code, *own_left(index)))

    total = lax.fori_loop(1, left_rounds, next_round, total)

    total = total.reshape(blocks, pair_rows, ab_cols)
    ids = jnp.arange(blocks)[:, None, None]
    total = total + jnp.where(ids == block, mine[None, :pair_rows], 0.0)
    total = total + jnp.where(ids == level * sides + 1 - side, mine[None, pair_rows:], 0.0)
    return reduce_to_owners(0.5 * total.reshape(blocks * pair_rows, ab_cols))


def solution(mesh):
    in_specs = (P("remap", None, "rep"), P("remap", "rep", None), P(), P())
    out_specs = P("remap", "rep")
    return jax.shard_map(body, mesh=mesh, in_specs=in_specs, out_specs=out_specs, check_vma=False)
```

```python
import functools

import jax
import jax.numpy as jnp
import numpy as np
from jax import lax
from jax.experimental import pallas as pl
from jax.experimental.pallas import tpu as pltpu
from jax.sharding import PartitionSpec as P

SLABS = 64
IRREPS = 8
BINS = 10
LEFT = 9
LEFT_MORE = 1
VMEM_BYTES = 48 * 1024 * 1024
BYTES_A_US = 3_600_000


def irrep_of(indices, table):
    matches = indices[:, None] == jnp.arange(table.shape[0], dtype=jnp.int32)[None, :]
    return jnp.sum(jnp.where(matches, table[None, :], 0), axis=1)


def sum_kernel(parts_ref, out_ref):
    rows, cols = out_ref.shape
    total = jnp.sum(parts_ref[...], axis=0)
    out_ref[...] = jnp.concatenate(
        [total[:, r * cols : (r + 1) * cols] for r in range(rows)], axis=0
    )


def reduce_to_owners(partial_term):
    remap, rep = lax.axis_size("remap"), lax.axis_size("rep")
    rows, cols = partial_term.shape
    blocks = partial_term.reshape(remap, rows // remap, rep, cols // rep)
    blocks = blocks.transpose(0, 2, 1, 3).reshape(remap * rep, 1, -1)
    arrived = lax.all_to_all(blocks, ("remap", "rep"), split_axis=0, concat_axis=0, tiled=True)
    return pl.pallas_call(
        sum_kernel,
        out_shape=jax.ShapeDtypeStruct((rows // remap, cols // rep), jnp.float32),
        name="sum_parts",
    )(arrived)


def first_plus_one(match):
    c_plus_one = jnp.arange(1, match.shape[1] + 1, dtype=jnp.int32)
    return jnp.sum(jnp.where(match, c_plus_one[None, :, None], 0), axis=1)


def takes(us):
    return pl.CostEstimate(flops=0, bytes_accessed=int(us * BYTES_A_US), transcendentals=0)


def whole(array):
    zeros = (0,) * array.ndim
    return pl.BlockSpec(array.shape, lambda *_: zeros)


def split_lanes(d_cols):
    main = d_cols // 128 * 128
    tail = d_cols - main
    pitch = -(-tail // 16) * 16
    return main, tail, pitch


def pack_kernel(irreps, slab, integrals, out_ref, rows, code_ref, arrived):
    c_rows, d_cols, ab = integrals.shape
    bins = out_ref.shape[0]
    virtual = irreps.shape[0]

    def fetch(c, i):
        return pltpu.make_async_copy(integrals.at[c], rows.at[i], arrived.at[i])

    c_first = lax.axis_index("remap") * c_rows

    def place(c, words):
        h = irreps[c_first + c]
        shift = (h & 3) * 8
        low = h < 4
        g = (jnp.where(low, words[0], words[1]) >> shift) & 255

        @pl.when(g < bins)
        def _():
            fetch(c, g * IRREPS + h).start()

        step = jnp.where(g < bins, jnp.int32(1) << shift, 0)
        return words[0] + jnp.where(low, step, 0), words[1] + jnp.where(low, 0, step)

    words = lax.fori_loop(0, c_rows, place, (jnp.int32(0), jnp.int32(0)), unroll=15)
    counts = [(words[h // 4] >> (h % 4 * 8)) & 255 for h in range(IRREPS)]

    pair = slab[0] * (virtual * virtual // SLABS)
    a_first = pair // virtual
    b_first = pair - a_first * virtual
    lane = lax.broadcasted_iota(jnp.int32, (1, ab), 1)

    def symmetry(k, sym):
        over = (b_first + k >= virtual).astype(jnp.int32)
        value = irreps[a_first + over] ^ irreps[b_first + k - over * virtual]
        return jnp.where(lane == k, value, sym)

    sym = lax.fori_loop(0, ab, symmetry, jnp.zeros((1, ab), jnp.int32), unroll=64)
    d_first = lax.axis_index("rep") * d_cols

    def code_row(d, carry):
        code_ref[pl.ds(d, 1), :] = sym ^ irreps[d_first + d]
        return carry

    lax.fori_loop(0, d_cols, code_row, 0, unroll=75)

    code = code_ref[...].astype(jnp.float32).astype(rows.dtype)

    def one(g, carry):
        for h in range(IRREPS):
            i = g * IRREPS + h

            @pl.when(g < counts[h])
            def _():
                fetch(0, i).wait()

            @pl.when(g >= counts[h])
            def _():
                rows[i] = jnp.zeros((d_cols, ab), rows.dtype)

        total = rows[g * IRREPS]
        for h in range(1, IRREPS):
            total = jnp.where(code == h, rows[g * IRREPS + h], total)
        out_ref[g, pl.ds(0, d_cols)] = total
        return carry

    lax.fori_loop(0, bins, one, 0)


def pack(integrals, irreps, slab):
    _, d_cols, ab = integrals.shape
    padded = -(-d_cols // 16) * 16
    out = jax.ShapeDtypeStruct((BINS, padded, ab), integrals.dtype)
    return pl.pallas_call(
        pack_kernel,
        out_shape=out,
        grid_spec=pltpu.PrefetchScalarGridSpec(
            num_scalar_prefetch=2,
            grid=(1,),
            in_specs=[pl.BlockSpec(memory_space=pl.ANY)],
            out_specs=whole(out),
            scratch_shapes=[
                pltpu.VMEM((BINS * IRREPS, d_cols, ab), integrals.dtype),
                pltpu.VMEM((d_cols, ab), jnp.int32),
                pltpu.SemaphoreType.DMA((BINS * IRREPS,)),
            ],
        ),
        cost_estimate=takes(4),
        compiler_params=pltpu.CompilerParams(vmem_limit_bytes=VMEM_BYTES),
        name="pack_bins",
    )(irreps, slab, integrals)


def route_kernel(firsts, width, c_at, blocks, rows_ref, *outs):
    base = blocks[pl.program_id(0)] * width
    pair_rows, d_cols = rows_ref.shape[1:]
    main, tail, pitch = split_lanes(d_cols)
    for first, out in zip(firsts, outs):

        def one(group, carry):
            tails = []
            for i in range(IRREPS):
                at = c_at[base + (first + group) * IRREPS + i]
                out[0, group, :, pl.ds(i * main, main)] = rows_ref[at, :, pl.ds(0, main)]
                end = rows_ref[at, :, pl.ds(main, tail)].astype(jnp.float32)
                tails += [end, jnp.zeros((pair_rows, pitch - tail), jnp.float32)]
            ends = jnp.concatenate([x for x in tails if x.shape[1]], axis=1)
            out[0, group, :, pl.ds(IRREPS * main, IRREPS * pitch)] = ends.astype(out.dtype)
            return carry

        lax.fori_loop(0, out.shape[1], one, 0)


def route(by_c, c_at, blocks, spans, c_rows, by_block):
    pair_rows, d_cols = by_c.shape[1:]
    steps = blocks.shape[0]
    main, _, pitch = split_lanes(d_cols)
    lanes = IRREPS * (main + pitch)
    at_block = lambda i, c_at, blocks: (blocks[i], 0, 0, 0)
    in_order = lambda i, c_at, blocks: (i, 0, 0, 0)
    return pl.pallas_call(
        functools.partial(route_kernel, [first for first, _ in spans], c_at.shape[1]),
        out_shape=[
            jax.ShapeDtypeStruct((steps, groups, pair_rows, lanes), by_c.dtype)
            for _, groups in spans
        ],
        grid_spec=pltpu.PrefetchScalarGridSpec(
            num_scalar_prefetch=2,
            grid=(steps,),
            in_specs=[
                pl.BlockSpec(
                    (c_rows, pair_rows, d_cols), lambda i, c_at, blocks: (blocks[i], 0, 0)
                )
            ],
            out_specs=[
                pl.BlockSpec((1, groups, pair_rows, lanes), at_block if by_block else in_order)
                for _, groups in spans
            ],
        ),
        cost_estimate=takes(0.1 * steps * sum(groups for _, groups in spans)),
        compiler_params=pltpu.CompilerParams(vmem_limit_bytes=VMEM_BYTES),
        name="route_rows",
    )(c_at.reshape(-1), blocks, by_c)


def chosen_rows(g, lo, size, own, other, level, other_level, irr_d, dtype):
    main, _, pitch = split_lanes(irr_d.shape[1])

    def lane(h):
        return h * main if lo < main else IRREPS * main + h * pitch

    sides = [
        [side[at, g, :, pl.ds(lane(h), size)].astype(jnp.float32) for h in range(IRREPS)]
        for side, at in ((own, level), (other, other_level))
    ]
    irr = irr_d[:, lo : lo + size]
    rows = []
    for s in range(IRREPS):
        for side in sides:
            value = side[s]
            for j in range(1, IRREPS):
                value = jnp.where(irr == j, side[s ^ j], value)
            rows.append(value)
    return jnp.concatenate(rows, axis=0).astype(dtype)


def spans_of(d_cols):
    main, tail, _ = split_lanes(d_cols)
    return [(0, main), (main, tail)] if tail else [(0, main)]


def add_bins(total, bins, own, other, level, other_level, irr_d):
    def one(g, carry):
        sum_ = total[...]
        for lo, size in spans_of(irr_d.shape[1]):
            lhs = chosen_rows(g, lo, size, own, other, level, other_level, irr_d, bins.dtype)
            sum_ += jnp.dot(lhs, bins[g, pl.ds(lo, size)], preferred_element_type=jnp.float32)
        total[...] = sum_
        return carry

    lax.fori_loop(0, bins.shape[0], one, 0)


def pick_symmetry(total, sym, rows):
    picked = jnp.zeros((rows, total.shape[1]), jnp.float32)
    for s in range(IRREPS):
        picked = jnp.where(sym == s, total[pl.ds(s * rows, rows), :], picked)
    return picked


def choose_kernel(places, n_other, info, irr_ref, own, *refs):
    others, out = refs[:n_other], refs[n_other]
    irr_d = irr_ref[...]
    level, first = jnp.maximum(info[places[0]], info[places[1]]), 0
    for other in others:
        last = first + other.shape[0]

        @pl.when((level >= first) & (level < last))
        def _():
            def one(g, carry):
                for lo, size in spans_of(irr_d.shape[1]):
                    out[g, :, pl.ds(lo, size)] = chosen_rows(
                        g, lo, size, own, other, level, level - first, irr_d, out.dtype
                    )
                return carry

            lax.fori_loop(0, out.shape[0], one, 0)

        first = last


def choose(places, own, other, info, irr_d):
    pair_rows, d_cols = irr_d.shape
    tensors = [irr_d, own, *other]
    return pl.pallas_call(
        functools.partial(choose_kernel, places, len(other)),
        out_shape=jax.ShapeDtypeStruct((BINS, IRREPS * 2 * pair_rows, d_cols), own.dtype),
        grid_spec=pltpu.PrefetchScalarGridSpec(
            num_scalar_prefetch=1,
            grid=(1,),
            in_specs=[pl.BlockSpec(memory_space=pltpu.VMEM)] * len(tensors),
            out_specs=pl.BlockSpec(memory_space=pltpu.VMEM),
        ),
        cost_estimate=takes(3),
        compiler_params=pltpu.CompilerParams(vmem_limit_bytes=VMEM_BYTES // 3),
        name="choose_rows",
    )(info, *tensors)


def last_kernel(places, info, sym_ref, chosen_ref, up, down, out, total, chosen, bins, arrived):
    rows = pltpu.make_async_copy(chosen_ref, chosen, arrived.at[0])
    rows.start()
    total[...] = jnp.zeros_like(total)
    for place, part in zip(places, (up, down)):

        @pl.when(info[place] >= 0)
        def _():
            copy = pltpu.make_async_copy(part, bins, arrived.at[1])
            copy.start()
            copy.wait()

    rows.wait()

    @pl.when(jnp.maximum(info[places[0]], info[places[1]]) >= 0)
    def _():
        sum_ = jnp.zeros(total.shape, jnp.float32)
        for g in range(bins.shape[0]):
            sum_ += jnp.dot(
                chosen[g], bins[g, pl.ds(0, chosen.shape[2])], preferred_element_type=jnp.float32
            )
        total[...] = sum_

    out[...] = pick_symmetry(total, sym_ref[...], out.shape[0])


def last_product(places, parts, chosen, info, sym):
    rows, ab = chosen.shape[1], sym.shape[1]
    out = jax.ShapeDtypeStruct((rows // IRREPS, ab), jnp.float32)
    return pl.pallas_call(
        functools.partial(last_kernel, places),
        out_shape=out,
        grid_spec=pltpu.PrefetchScalarGridSpec(
            num_scalar_prefetch=1,
            grid=(1,),
            in_specs=[whole(sym)] + [pl.BlockSpec(memory_space=pl.ANY)] * 3,
            out_specs=whole(out),
            scratch_shapes=[
                pltpu.VMEM((rows, ab), jnp.float32),
                pltpu.VMEM(chosen.shape, chosen.dtype),
                pltpu.VMEM(parts[0].shape, parts[0].dtype),
                pltpu.SemaphoreType.DMA((2,)),
            ],
        ),
        cost_estimate=takes(2),
        compiler_params=pltpu.CompilerParams(vmem_limit_bytes=VMEM_BYTES),
        name="last_product",
    )(info, sym, chosen, *parts)


def bins_kernel(places, n_other, info, irr_ref, sym_ref, own, *refs):
    others, refs = refs[:n_other], refs[n_other:]
    bins, (out, total) = refs[:-2], refs[-2:]
    irr_d, sym = irr_ref[...], sym_ref[...]
    total[...] = jnp.zeros_like(total)
    for place, part in zip(places, bins):
        level, first = info[place], 0
        for other in others:
            last = first + other.shape[0]

            @pl.when((level >= first) & (level < last))
            def _():
                add_bins(total, part, own, other, level, level - first, irr_d)

            first = last

    out[...] = pick_symmetry(total, sym, out.shape[0])


def bins_product(places, parts, own, other, info, irr_d, sym):
    pair_rows, ab = irr_d.shape[0], sym.shape[1]
    out = jax.ShapeDtypeStruct((2 * pair_rows, ab), jnp.float32)
    tensors = [irr_d, sym, own, *other, *parts]
    return pl.pallas_call(
        functools.partial(bins_kernel, places, len(other)),
        out_shape=out,
        grid_spec=pltpu.PrefetchScalarGridSpec(
            num_scalar_prefetch=1,
            grid=(1,),
            in_specs=[pl.BlockSpec(memory_space=pltpu.VMEM)] * len(tensors),
            out_specs=whole(out),
            scratch_shapes=[pltpu.VMEM((IRREPS * 2 * pair_rows, ab), jnp.float32)],
        ),
        cost_estimate=takes(3),
        compiler_params=pltpu.CompilerParams(vmem_limit_bytes=VMEM_BYTES // 3),
        name="bins_product",
    )(info, *tensors)


def left_rows_kernel(slots, irreps, code_ref, integrals, out_ref, rows, arrived):
    group = pl.program_id(0)
    d_cols, ab = code_ref.shape
    main, tail, pitch = split_lanes(d_cols)

    def fetch(i):
        c = jnp.maximum(slots[i] - 1, 0)
        return pltpu.make_async_copy(integrals.at[c], rows.at[i], arrived.at[i])

    def start(i, carry):
        fetch(i).start()
        return carry

    @pl.when(group == 0)
    def _():
        lax.fori_loop(0, rows.shape[0], start, 0)

    code = code_ref[...]
    for h in range(IRREPS):
        i = group * IRREPS + h
        fetch(i).wait()
        irrep = jnp.where(slots[i] > 0, irreps[i], IRREPS)
        row = jnp.where(code == irrep, rows[i].astype(jnp.float32), 0.0)
        out_ref[0, pl.ds(h * main, main)] = row[:main].astype(out_ref.dtype)
        if tail:
            end = row[main:]
            if pitch > tail:
                end = jnp.concatenate([end, jnp.zeros((pitch - tail, ab), jnp.float32)], axis=0)
            out_ref[0, pl.ds(IRREPS * main + h * pitch, pitch)] = end.astype(out_ref.dtype)


def left_rows(integrals, code, slots, irreps):
    d_cols, ab = code.shape
    count = slots.shape[0]
    main, _, pitch = split_lanes(d_cols)
    depth = IRREPS * (main + pitch)
    return pl.pallas_call(
        left_rows_kernel,
        out_shape=jax.ShapeDtypeStruct((count // IRREPS, depth, ab), integrals.dtype),
        grid_spec=pltpu.PrefetchScalarGridSpec(
            num_scalar_prefetch=2,
            grid=(count // IRREPS,),
            in_specs=[whole(code), pl.BlockSpec(memory_space=pl.ANY)],
            out_specs=pl.BlockSpec((1, depth, ab), lambda i, *_: (i, 0, 0)),
            scratch_shapes=[
                pltpu.VMEM((count, d_cols, ab), integrals.dtype),
                pltpu.SemaphoreType.DMA((count,)),
            ],
        ),
        cost_estimate=takes(5),
        compiler_params=pltpu.CompilerParams(vmem_limit_bytes=VMEM_BYTES),
        name="left_rows",
    )(slots, irreps, code, integrals)


def left_kernel(amp_ref, row_ref, out_ref, amps, rows, amps_here, rows_here):
    sources, groups, pair_rows, depth = amp_ref.shape
    first = groups // 2
    halves = [(0, first), (first, groups - first)] if first else [(0, groups)]
    halves = [(at, pl.ds(lo, size), lo, size) for at, (lo, size) in enumerate(halves)]
    copies = []
    for at, span, lo, size in halves:
        copies.append(
            [
                pltpu.make_async_copy(
                    amp_ref.at[source, span], amps.at[source, span], amps_here.at[at, source]
                )
                for source in range(sources)
            ]
            + [
                pltpu.make_async_copy(row_ref.at[group], rows.at[group], rows_here.at[group])
                for group in range(lo, lo + size)
            ]
        )
    for half in copies:
        for copy in half:
            copy.start()
    total = jnp.zeros(out_ref.shape, jnp.float32)
    for half, (_, _, lo, size) in zip(copies, halves):
        for copy in half:
            copy.wait()
        for group in range(lo, lo + size):
            lhs = amps[:, group].astype(jnp.float32).reshape(sources * pair_rows, depth)
            total += jnp.dot(
                lhs.astype(rows.dtype), rows[group], preferred_element_type=jnp.float32
            )
    out_ref[...] = total


def left_product(amps, rows):
    sources, groups, pair_rows, depth = amps.shape
    ab = rows.shape[2]
    return pl.pallas_call(
        left_kernel,
        out_shape=jax.ShapeDtypeStruct((sources * pair_rows, ab), jnp.float32),
        in_specs=[pl.BlockSpec(memory_space=pl.ANY)] * 2,
        out_specs=pl.BlockSpec(memory_space=pltpu.VMEM),
        scratch_shapes=[
            pltpu.VMEM(amps.shape, amps.dtype),
            pltpu.VMEM(rows.shape, rows.dtype),
            pltpu.SemaphoreType.DMA((2, sources)),
            pltpu.SemaphoreType.DMA((groups,)),
        ],
        cost_estimate=takes(5),
        compiler_params=pltpu.CompilerParams(vmem_limit_bytes=VMEM_BYTES),
        name="left_product",
    )(amps, rows)


def body(amplitudes, integrals, orbital_irreps, slab_index):
    c_rows, d_cols, ab_cols = integrals.shape
    pair_rows = amplitudes.shape[0]
    virtual = orbital_irreps.shape[0]
    blocks = lax.axis_size("remap")
    sides = 2
    levels = blocks // sides
    assert levels >= 2 and blocks == levels * sides
    block = lax.axis_index("remap")
    level, side = block // sides, block % sides
    slots = (BINS + LEFT) * IRREPS

    bins = pack(integrals, orbital_irreps, slab_index)
    amplitudes, orbital_irreps, bins = lax.optimization_barrier((amplitudes, orbital_irreps, bins))

    earlier = jnp.arange(c_rows)[:, None] < jnp.arange(c_rows)[None, :]

    def places_of(irr):
        alike = (irr[:, :, None] == irr[:, None, :]) & earlier[None]
        rank = jnp.sum(alike.astype(jnp.int32), axis=1)
        over = rank >= BINS
        left_rank = jnp.sum((over[:, :, None] & earlier[None]).astype(jnp.int32), axis=1)
        return jnp.where(over, BINS * IRREPS + left_rank, rank * IRREPS + irr)

    def table(places, first, count):
        wanted = first + jnp.arange(count, dtype=jnp.int32)
        return first_plus_one(places[:, :, None] == wanted[None, None, :])

    own_irr = lax.dynamic_slice_in_dim(orbital_irreps, block * c_rows, c_rows, 0)
    own_places = places_of(own_irr[None])

    def own_left(first, count):
        match = own_places[0][:, None] == first + jnp.arange(count, dtype=jnp.int32)[None, :]
        irreps = jnp.sum(jnp.where(match, own_irr[:, None], 0), axis=0)
        return first_plus_one(match[None])[0], irreps

    irr_d = lax.dynamic_slice_in_dim(orbital_irreps, lax.axis_index("rep") * d_cols, d_cols, 0)
    stride = virtual * virtual // SLABS
    pair_ab = slab_index[0] * stride + jnp.arange(ab_cols, dtype=jnp.int32)
    sym_ab = jnp.bitwise_xor(
        irrep_of(pair_ab // virtual, orbital_irreps), irrep_of(pair_ab % virtual, orbital_irreps)
    )
    code = jnp.bitwise_xor(irr_d[:, None], sym_ab[None, :])
    irr_rows = jnp.broadcast_to(irr_d[None, :], (pair_rows, d_cols))

    order = [1, 0] + list(range(2, levels))

    def at_level(z, a):
        return a if z < levels // 2 else levels - 1 - a

    plan = []
    for z in range(levels):
        for b in range(sides):
            row = [at_level(z, a) * sides + c for c in (1 - b, b) for a in order]
            for t in range(levels):
                for a in (z - t, z + t):
                    row.append(order.index(at_level(z, a)) if 0 <= a < levels else -1)
            plan.append(row)
    info = lax.dynamic_index_in_dim(jnp.asarray(np.array(plan, np.int32)), block, 0, False)

    by_c = amplitudes.transpose(1, 0, 2)

    def hops(pairs, swap):
        return [
            (a * sides + b, c * sides + (sides - 1 - b if swap else b))
            for a, c in pairs
            for b in range(sides)
        ]

    rounds = [(bins, bins)]
    for t in range(1, levels):
        up = [(z, z + 1) for z in range(t - 1, levels - 1)]
        down = [(levels - 1 - a, levels - 1 - c) for a, c in up]
        rounds.append(
            (
                lax.ppermute(rounds[-1][0], "remap", hops(up, False)),
                lax.ppermute(rounds[-1][1], "remap", hops(down, False)),
            )
        )
    places = places_of(orbital_irreps.reshape(blocks, c_rows))
    more = LEFT_MORE * IRREPS
    more_rounds = jnp.maximum(jnp.max(places) - slots + more, 0) // more
    c_at = jnp.maximum(table(places, 0, slots) - 1, 0)
    in_bins = [(0, BINS)]
    split = levels // 2
    stay = hops([(z, z) for z in range(levels)], True)
    def left_term(sent, rows):
        arrived = lax.all_to_all(sent, "remap", split_axis=0, concat_axis=0, tiled=True)
        return left_product(arrived, rows)

    (near,) = route(by_c, c_at, info[:split], in_bins, c_rows, False)
    near = lax.ppermute(near, "remap", stay)
    by_c, rounds[1] = lax.optimization_barrier((by_c, rounds[1]))
    every = jnp.arange(blocks, dtype=jnp.int32)
    (sent,) = route(by_c, c_at, every, [(BINS, LEFT)], c_rows, True)
    (far,) = route(by_c, c_at, info[split:levels], in_bins, c_rows, False)
    (own,) = route(by_c, c_at, info[levels:blocks], in_bins, c_rows, False)
    left_at = own_left(BINS * IRREPS, LEFT * IRREPS)
    sent, left_at, near, rounds[2], code, irr_rows, sym_ab = lax.optimization_barrier(
        (sent, left_at, near, rounds[2], code, irr_rows, sym_ab)
    )
    other = [near, lax.ppermute(far, "remap", stay)]
    total = left_term(sent, left_rows(integrals, code, *left_at))
    rounds[-1], total = lax.optimization_barrier((rounds[-1], total))
    mine = 0
    for t, parts in enumerate(rounds):
        ways = [blocks + 2 * t, blocks + 2 * t + 1]
        if t == 0:
            ways, parts = ways[:1], parts[:1]
        reach = max(row[way] for row in plan for way in ways)
        if t == levels - 1:
            chosen = choose(ways, own, other, info, irr_rows)
            mine += last_product(ways, parts, chosen, info, sym_ab[None, :])
            continue
        mine += bins_product(ways, parts, own, other[: 1 + (reach >= split)], info, irr_rows, sym_ab[None, :])

    def next_round(index, total):
        first = slots + index * more
        c_at = jnp.maximum(table(places, first, more) - 1, 0)
        (sent,) = route(by_c, c_at, every, [(0, LEFT_MORE)], c_rows, True)
        return total + left_term(sent, left_rows(integrals, code, *own_left(first, more)))

    total = lax.fori_loop(0, more_rounds, next_round, total)

    total = total.reshape(blocks, pair_rows, ab_cols)
    ids = jnp.arange(blocks)[:, None, None]
    total = total + jnp.where(ids == block, mine[None, :pair_rows], 0.0)
    total = total + jnp.where(ids == level * sides + 1 - side, mine[None, pair_rows:], 0.0)
    return reduce_to_owners(0.5 * total.reshape(blocks * pair_rows, ab_cols))


def solution(mesh):
    in_specs = (P("remap", None, "rep"), P("remap", "rep", None), P(), P())
    out_specs = P("remap", "rep")
    return jax.shard_map(body, mesh=mesh, in_specs=in_specs, out_specs=out_specs, check_vma=False)
```

```python
import functools

import jax
import jax.numpy as jnp
import numpy as np
from jax import lax
from jax.experimental import pallas as pl
from jax.experimental.pallas import tpu as pltpu
from jax.sharding import PartitionSpec as P

SLABS = 64
IRREPS = 8
BINS = 10
LEFT = 9
LEFT_MORE = 1
VMEM_BYTES = 48 * 1024 * 1024
BYTES_A_US = 3_600_000


def irrep_of(indices, table):
    matches = indices[:, None] == jnp.arange(table.shape[0], dtype=jnp.int32)[None, :]
    return jnp.sum(jnp.where(matches, table[None, :], 0), axis=1)


def sum_kernel(parts_ref, out_ref):
    rows, cols = out_ref.shape
    total = jnp.sum(parts_ref[...], axis=0)
    out_ref[...] = jnp.concatenate(
        [total[:, r * cols : (r + 1) * cols] for r in range(rows)], axis=0
    )


def reduce_to_owners(partial_term):
    remap, rep = lax.axis_size("remap"), lax.axis_size("rep")
    rows, cols = partial_term.shape
    blocks = partial_term.reshape(remap, rows // remap, rep, cols // rep)
    blocks = blocks.transpose(0, 2, 1, 3).reshape(remap * rep, 1, -1)
    arrived = lax.all_to_all(blocks, ("remap", "rep"), split_axis=0, concat_axis=0, tiled=True)
    return pl.pallas_call(
        sum_kernel,
        out_shape=jax.ShapeDtypeStruct((rows // remap, cols // rep), jnp.float32),
        name="sum_parts",
    )(arrived)


def first_plus_one(match):
    c_plus_one = jnp.arange(1, match.shape[1] + 1, dtype=jnp.int32)
    return jnp.sum(jnp.where(match, c_plus_one[None, :, None], 0), axis=1)


def takes(us):
    return pl.CostEstimate(flops=0, bytes_accessed=int(us * BYTES_A_US), transcendentals=0)


def whole(array):
    zeros = (0,) * array.ndim
    return pl.BlockSpec(array.shape, lambda *_: zeros)


def split_lanes(d_cols):
    main = d_cols // 128 * 128
    tail = d_cols - main
    pitch = -(-tail // 16) * 16
    return main, tail, pitch


def pack_kernel(irreps, slab, integrals, out_ref, rows, code_ref, arrived):
    c_rows, d_cols, ab = integrals.shape
    bins = out_ref.shape[0]
    virtual = irreps.shape[0]

    def fetch(c, i):
        return pltpu.make_async_copy(integrals.at[c], rows.at[i], arrived.at[i])

    c_first = lax.axis_index("remap") * c_rows

    def place(c, words):
        h = irreps[c_first + c]
        shift = (h & 3) * 8
        low = h < 4
        g = (jnp.where(low, words[0], words[1]) >> shift) & 255

        @pl.when(g < bins)
        def _():
            fetch(c, g * IRREPS + h).start()

        step = jnp.where(g < bins, jnp.int32(1) << shift, 0)
        return words[0] + jnp.where(low, step, 0), words[1] + jnp.where(low, 0, step)

    words = lax.fori_loop(0, c_rows, place, (jnp.int32(0), jnp.int32(0)), unroll=15)
    counts = [(words[h // 4] >> (h % 4 * 8)) & 255 for h in range(IRREPS)]

    pair = slab[0] * (virtual * virtual // SLABS)
    a_first = pair // virtual
    b_first = pair - a_first * virtual
    lane = lax.broadcasted_iota(jnp.int32, (1, ab), 1)

    def symmetry(k, sym):
        over = (b_first + k >= virtual).astype(jnp.int32)
        value = irreps[a_first + over] ^ irreps[b_first + k - over * virtual]
        return jnp.where(lane == k, value, sym)

    sym = lax.fori_loop(0, ab, symmetry, jnp.zeros((1, ab), jnp.int32), unroll=64)
    d_first = lax.axis_index("rep") * d_cols

    def code_row(d, carry):
        code_ref[pl.ds(d, 1), :] = sym ^ irreps[d_first + d]
        return carry

    lax.fori_loop(0, d_cols, code_row, 0, unroll=75)

    code = code_ref[...].astype(jnp.float32).astype(rows.dtype)

    def one(g, carry):
        for h in range(IRREPS):
            i = g * IRREPS + h

            @pl.when(g < counts[h])
            def _():
                fetch(0, i).wait()

            @pl.when(g >= counts[h])
            def _():
                rows[i] = jnp.zeros((d_cols, ab), rows.dtype)

        total = rows[g * IRREPS]
        for h in range(1, IRREPS):
            total = jnp.where(code == h, rows[g * IRREPS + h], total)
        out_ref[g, pl.ds(0, d_cols)] = total
        return carry

    lax.fori_loop(0, bins, one, 0)


def pack(integrals, irreps, slab):
    _, d_cols, ab = integrals.shape
    padded = -(-d_cols // 16) * 16
    out = jax.ShapeDtypeStruct((BINS, padded, ab), integrals.dtype)
    return pl.pallas_call(
        pack_kernel,
        out_shape=out,
        grid_spec=pltpu.PrefetchScalarGridSpec(
            num_scalar_prefetch=2,
            grid=(1,),
            in_specs=[pl.BlockSpec(memory_space=pl.ANY)],
            out_specs=whole(out),
            scratch_shapes=[
                pltpu.VMEM((BINS * IRREPS, d_cols, ab), integrals.dtype),
                pltpu.VMEM((d_cols, ab), jnp.int32),
                pltpu.SemaphoreType.DMA((BINS * IRREPS,)),
            ],
        ),
        cost_estimate=takes(4),
        compiler_params=pltpu.CompilerParams(vmem_limit_bytes=VMEM_BYTES),
        name="pack_bins",
    )(irreps, slab, integrals)


def route_kernel(firsts, width, c_at, blocks, rows_ref, *outs):
    base = blocks[pl.program_id(0)] * width
    pair_rows, d_cols = rows_ref.shape[1:]
    main, tail, pitch = split_lanes(d_cols)
    for first, out in zip(firsts, outs):

        def one(group, carry):
            tails = []
            for i in range(IRREPS):
                at = c_at[base + (first + group) * IRREPS + i]
                out[0, group, :, pl.ds(i * main, main)] = rows_ref[at, :, pl.ds(0, main)]
                end = rows_ref[at, :, pl.ds(main, tail)].astype(jnp.float32)
                tails += [end, jnp.zeros((pair_rows, pitch - tail), jnp.float32)]
            ends = jnp.concatenate([x for x in tails if x.shape[1]], axis=1)
            out[0, group, :, pl.ds(IRREPS * main, IRREPS * pitch)] = ends.astype(out.dtype)
            return carry

        lax.fori_loop(0, out.shape[1], one, 0)


def route(by_c, c_at, blocks, spans, c_rows, by_block):
    pair_rows, d_cols = by_c.shape[1:]
    steps = blocks.shape[0]
    main, _, pitch = split_lanes(d_cols)
    lanes = IRREPS * (main + pitch)
    at_block = lambda i, c_at, blocks: (blocks[i], 0, 0, 0)
    in_order = lambda i, c_at, blocks: (i, 0, 0, 0)
    return pl.pallas_call(
        functools.partial(route_kernel, [first for first, _ in spans], c_at.shape[1]),
        out_shape=[
            jax.ShapeDtypeStruct((steps, groups, pair_rows, lanes), by_c.dtype)
            for _, groups in spans
        ],
        grid_spec=pltpu.PrefetchScalarGridSpec(
            num_scalar_prefetch=2,
            grid=(steps,),
            in_specs=[
                pl.BlockSpec(
                    (c_rows, pair_rows, d_cols), lambda i, c_at, blocks: (blocks[i], 0, 0)
                )
            ],
            out_specs=[
                pl.BlockSpec((1, groups, pair_rows, lanes), at_block if by_block else in_order)
                for _, groups in spans
            ],
        ),
        cost_estimate=takes(0.1 * steps * sum(groups for _, groups in spans)),
        compiler_params=pltpu.CompilerParams(vmem_limit_bytes=VMEM_BYTES),
        name="route_rows",
    )(c_at.reshape(-1), blocks, by_c)


def chosen_rows(g, lo, size, own, other, level, other_level, irr_d, dtype):
    main, _, pitch = split_lanes(irr_d.shape[1])

    def lane(h):
        return h * main if lo < main else IRREPS * main + h * pitch

    sides = [
        [side[at, g, :, pl.ds(lane(h), size)].astype(jnp.float32) for h in range(IRREPS)]
        for side, at in ((own, level), (other, other_level))
    ]
    irr = irr_d[:, lo : lo + size]
    rows = []
    for s in range(IRREPS):
        for side in sides:
            value = side[s]
            for j in range(1, IRREPS):
                value = jnp.where(irr == j, side[s ^ j], value)
            rows.append(value)
    return jnp.concatenate(rows, axis=0).astype(dtype)


def spans_of(d_cols):
    main, tail, _ = split_lanes(d_cols)
    return [(0, main), (main, tail)] if tail else [(0, main)]


def add_bins(total, bins, own, other, level, other_level, irr_d):
    def one(g, carry):
        sum_ = total[...]
        for lo, size in spans_of(irr_d.shape[1]):
            lhs = chosen_rows(g, lo, size, own, other, level, other_level, irr_d, bins.dtype)
            sum_ += jnp.dot(lhs, bins[g, pl.ds(lo, size)], preferred_element_type=jnp.float32)
        total[...] = sum_
        return carry

    lax.fori_loop(0, bins.shape[0], one, 0)


def pick_symmetry(total, sym, rows):
    picked = jnp.zeros((rows, total.shape[1]), jnp.float32)
    for s in range(IRREPS):
        picked = jnp.where(sym == s, total[pl.ds(s * rows, rows), :], picked)
    return picked


def choose_kernel(places, n_other, info, irr_ref, own, *refs):
    others, out = refs[:n_other], refs[n_other]
    irr_d = irr_ref[...]
    level, first = jnp.maximum(info[places[0]], info[places[1]]), 0
    for other in others:
        last = first + other.shape[0]

        @pl.when((level >= first) & (level < last))
        def _():
            def one(g, carry):
                for lo, size in spans_of(irr_d.shape[1]):
                    out[g, :, pl.ds(lo, size)] = chosen_rows(
                        g, lo, size, own, other, level, level - first, irr_d, out.dtype
                    )
                return carry

            lax.fori_loop(0, out.shape[0], one, 0)

        first = last


def choose(places, own, other, info, irr_d):
    pair_rows, d_cols = irr_d.shape
    tensors = [irr_d, own, *other]
    return pl.pallas_call(
        functools.partial(choose_kernel, places, len(other)),
        out_shape=jax.ShapeDtypeStruct((BINS, IRREPS * 2 * pair_rows, d_cols), own.dtype),
        grid_spec=pltpu.PrefetchScalarGridSpec(
            num_scalar_prefetch=1,
            grid=(1,),
            in_specs=[pl.BlockSpec(memory_space=pltpu.VMEM)] * len(tensors),
            out_specs=pl.BlockSpec(memory_space=pltpu.VMEM),
        ),
        cost_estimate=takes(3),
        compiler_params=pltpu.CompilerParams(vmem_limit_bytes=VMEM_BYTES // 3),
        name="choose_rows",
    )(info, *tensors)


def last_kernel(places, info, sym_ref, before_ref, chosen_ref, up, down, out, total, chosen, bins, arrived):
    rows = pltpu.make_async_copy(chosen_ref, chosen, arrived.at[0])
    rows.start()
    total[...] = jnp.zeros_like(total)
    for place, part in zip(places, (up, down)):

        @pl.when(info[place] >= 0)
        def _():
            copy = pltpu.make_async_copy(part, bins, arrived.at[1])
            copy.start()
            copy.wait()

    rows.wait()

    @pl.when(jnp.maximum(info[places[0]], info[places[1]]) >= 0)
    def _():
        sum_ = jnp.zeros(total.shape, jnp.float32)
        for g in range(bins.shape[0]):
            sum_ += jnp.dot(
                chosen[g], bins[g, pl.ds(0, chosen.shape[2])], preferred_element_type=jnp.float32
            )
        total[...] = sum_

    out[...] = before_ref[...] + pick_symmetry(total, sym_ref[...], out.shape[0])


def last_product(places, parts, before, chosen, info, sym):
    rows, ab = chosen.shape[1], sym.shape[1]
    out = jax.ShapeDtypeStruct((rows // IRREPS, ab), jnp.float32)
    return pl.pallas_call(
        functools.partial(last_kernel, places),
        out_shape=out,
        grid_spec=pltpu.PrefetchScalarGridSpec(
            num_scalar_prefetch=1,
            grid=(1,),
            in_specs=[whole(sym), whole(before)] + [pl.BlockSpec(memory_space=pl.ANY)] * 3,
            out_specs=whole(out),
            scratch_shapes=[
                pltpu.VMEM((rows, ab), jnp.float32),
                pltpu.VMEM(chosen.shape, chosen.dtype),
                pltpu.VMEM(parts[0].shape, parts[0].dtype),
                pltpu.SemaphoreType.DMA((2,)),
            ],
        ),
        cost_estimate=takes(2),
        compiler_params=pltpu.CompilerParams(vmem_limit_bytes=VMEM_BYTES),
        name="last_product",
    )(info, sym, before, chosen, *parts)


def bins_kernel(places, n_other, info, irr_ref, sym_ref, own_ref, *refs):
    other_refs, refs = refs[:n_other], refs[n_other:]
    bins_refs, (out, total, own, other, bins, arrived) = refs[:-6], refs[-6:]
    irr_d, sym = irr_ref[...], sym_ref[...]

    def own_copy(way, level):
        return pltpu.make_async_copy(own_ref.at[level], own.at[way], arrived.at[way, 0])

    def other_copy(way, ref, level):
        return pltpu.make_async_copy(ref.at[level], other.at[way], arrived.at[way, 1])

    def bins_copy(way):
        return pltpu.make_async_copy(bins_refs[way], bins.at[way], arrived.at[way, 2])

    for way, place in enumerate(places):
        level, first = info[place], 0

        @pl.when(level >= 0)
        def _():
            own_copy(way, level).start()
            bins_copy(way).start()

        for ref in other_refs:
            last = first + ref.shape[0]

            @pl.when((level >= first) & (level < last))
            def _():
                other_copy(way, ref, level - first).start()

            first = last

    total[...] = jnp.zeros_like(total)
    for way, place in enumerate(places):

        @pl.when(info[place] >= 0)
        def _():
            own_copy(way, 0).wait()
            other_copy(way, other_refs[0], 0).wait()
            bins_copy(way).wait()
            add_bins(total, bins.at[way], own, other, way, way, irr_d)

    out[...] = pick_symmetry(total, sym, out.shape[0])


def bins_product(places, parts, own, other, info, irr_d, sym):
    pair_rows, ab = irr_d.shape[0], sym.shape[1]
    out = jax.ShapeDtypeStruct((2 * pair_rows, ab), jnp.float32)
    tensors = [own, *other, *parts]
    ways = len(parts)
    return pl.pallas_call(
        functools.partial(bins_kernel, places, len(other)),
        out_shape=out,
        grid_spec=pltpu.PrefetchScalarGridSpec(
            num_scalar_prefetch=1,
            grid=(1,),
            in_specs=[whole(irr_d), whole(sym)]
            + [pl.BlockSpec(memory_space=pl.ANY)] * len(tensors),
            out_specs=whole(out),
            scratch_shapes=[
                pltpu.VMEM((IRREPS * 2 * pair_rows, ab), jnp.float32),
                pltpu.VMEM((ways, *own.shape[1:]), own.dtype),
                pltpu.VMEM((ways, *own.shape[1:]), own.dtype),
                pltpu.VMEM((ways, *parts[0].shape), parts[0].dtype),
                pltpu.SemaphoreType.DMA((ways, 3)),
            ],
        ),
        cost_estimate=takes(3),
        compiler_params=pltpu.CompilerParams(vmem_limit_bytes=VMEM_BYTES),
        name="bins_product",
    )(info, irr_d, sym, *tensors)


def left_rows_kernel(slots, irreps, code_ref, integrals, out_ref, rows, arrived):
    group = pl.program_id(0)
    d_cols, ab = code_ref.shape
    main, tail, pitch = split_lanes(d_cols)

    def fetch(i):
        c = jnp.maximum(slots[i] - 1, 0)
        return pltpu.make_async_copy(integrals.at[c], rows.at[i], arrived.at[i])

    def start(i, carry):
        fetch(i).start()
        return carry

    @pl.when(group == 0)
    def _():
        lax.fori_loop(0, rows.shape[0], start, 0)

    code = code_ref[...]
    for h in range(IRREPS):
        i = group * IRREPS + h
        fetch(i).wait()
        irrep = jnp.where(slots[i] > 0, irreps[i], IRREPS)
        row = jnp.where(code == irrep, rows[i].astype(jnp.float32), 0.0)
        out_ref[0, pl.ds(h * main, main)] = row[:main].astype(out_ref.dtype)
        if tail:
            end = row[main:]
            if pitch > tail:
                end = jnp.concatenate([end, jnp.zeros((pitch - tail, ab), jnp.float32)], axis=0)
            out_ref[0, pl.ds(IRREPS * main + h * pitch, pitch)] = end.astype(out_ref.dtype)


def left_rows(integrals, code, slots, irreps):
    d_cols, ab = code.shape
    count = slots.shape[0]
    main, _, pitch = split_lanes(d_cols)
    depth = IRREPS * (main + pitch)
    return pl.pallas_call(
        left_rows_kernel,
        out_shape=jax.ShapeDtypeStruct((count // IRREPS, depth, ab), integrals.dtype),
        grid_spec=pltpu.PrefetchScalarGridSpec(
            num_scalar_prefetch=2,
            grid=(count // IRREPS,),
            in_specs=[whole(code), pl.BlockSpec(memory_space=pl.ANY)],
            out_specs=pl.BlockSpec((1, depth, ab), lambda i, *_: (i, 0, 0)),
            scratch_shapes=[
                pltpu.VMEM((count, d_cols, ab), integrals.dtype),
                pltpu.SemaphoreType.DMA((count,)),
            ],
        ),
        cost_estimate=takes(5),
        compiler_params=pltpu.CompilerParams(vmem_limit_bytes=VMEM_BYTES),
        name="left_rows",
    )(slots, irreps, code, integrals)


def left_kernel(amp_ref, row_ref, out_ref, amps, rows, amps_here, rows_here):
    sources, groups, pair_rows, depth = amp_ref.shape
    first = groups // 2
    halves = [(0, first), (first, groups - first)] if first else [(0, groups)]
    halves = [(at, pl.ds(lo, size), lo, size) for at, (lo, size) in enumerate(halves)]
    copies = []
    for at, span, lo, size in halves:
        copies.append(
            [
                pltpu.make_async_copy(
                    amp_ref.at[source, span], amps.at[source, span], amps_here.at[at, source]
                )
                for source in range(sources)
            ]
            + [
                pltpu.make_async_copy(row_ref.at[group], rows.at[group], rows_here.at[group])
                for group in range(lo, lo + size)
            ]
        )
    for half in copies:
        for copy in half:
            copy.start()
    total = jnp.zeros(out_ref.shape, jnp.float32)
    for half, (_, _, lo, size) in zip(copies, halves):
        for copy in half:
            copy.wait()
        for group in range(lo, lo + size):
            lhs = amps[:, group].astype(jnp.float32).reshape(sources * pair_rows, depth)
            total += jnp.dot(
                lhs.astype(rows.dtype), rows[group], preferred_element_type=jnp.float32
            )
    out_ref[...] = total


def left_product(amps, rows):
    sources, groups, pair_rows, depth = amps.shape
    ab = rows.shape[2]
    return pl.pallas_call(
        left_kernel,
        out_shape=jax.ShapeDtypeStruct((sources * pair_rows, ab), jnp.float32),
        in_specs=[pl.BlockSpec(memory_space=pl.ANY)] * 2,
        out_specs=pl.BlockSpec(memory_space=pltpu.VMEM),
        scratch_shapes=[
            pltpu.VMEM(amps.shape, amps.dtype),
            pltpu.VMEM(rows.shape, rows.dtype),
            pltpu.SemaphoreType.DMA((2, sources)),
            pltpu.SemaphoreType.DMA((groups,)),
        ],
        cost_estimate=takes(5),
        compiler_params=pltpu.CompilerParams(vmem_limit_bytes=VMEM_BYTES),
        name="left_product",
    )(amps, rows)


def body(amplitudes, integrals, orbital_irreps, slab_index):
    c_rows, d_cols, ab_cols = integrals.shape
    pair_rows = amplitudes.shape[0]
    virtual = orbital_irreps.shape[0]
    blocks = lax.axis_size("remap")
    sides = 2
    levels = blocks // sides
    assert levels >= 2 and blocks == levels * sides
    block = lax.axis_index("remap")
    level, side = block // sides, block % sides
    slots = (BINS + LEFT) * IRREPS

    bins = pack(integrals, orbital_irreps, slab_index)
    amplitudes, orbital_irreps, bins = lax.optimization_barrier((amplitudes, orbital_irreps, bins))

    earlier = jnp.arange(c_rows)[:, None] < jnp.arange(c_rows)[None, :]

    def places_of(irr):
        alike = (irr[:, :, None] == irr[:, None, :]) & earlier[None]
        rank = jnp.sum(alike.astype(jnp.int32), axis=1)
        over = rank >= BINS
        left_rank = jnp.sum((over[:, :, None] & earlier[None]).astype(jnp.int32), axis=1)
        return jnp.where(over, BINS * IRREPS + left_rank, rank * IRREPS + irr)

    def table(places, first, count):
        wanted = first + jnp.arange(count, dtype=jnp.int32)
        return first_plus_one(places[:, :, None] == wanted[None, None, :])

    own_irr = lax.dynamic_slice_in_dim(orbital_irreps, block * c_rows, c_rows, 0)
    own_places = places_of(own_irr[None])

    def own_left(first, count):
        match = own_places[0][:, None] == first + jnp.arange(count, dtype=jnp.int32)[None, :]
        irreps = jnp.sum(jnp.where(match, own_irr[:, None], 0), axis=0)
        return first_plus_one(match[None])[0], irreps

    irr_d = lax.dynamic_slice_in_dim(orbital_irreps, lax.axis_index("rep") * d_cols, d_cols, 0)
    stride = virtual * virtual // SLABS
    pair_ab = slab_index[0] * stride + jnp.arange(ab_cols, dtype=jnp.int32)
    sym_ab = jnp.bitwise_xor(
        irrep_of(pair_ab // virtual, orbital_irreps), irrep_of(pair_ab % virtual, orbital_irreps)
    )
    code = jnp.bitwise_xor(irr_d[:, None], sym_ab[None, :])
    irr_rows = jnp.broadcast_to(irr_d[None, :], (pair_rows, d_cols))

    order = [1, 0] + list(range(2, levels))

    def at_level(z, a):
        return a if z < levels // 2 else levels - 1 - a

    plan = []
    for z in range(levels):
        for b in range(sides):
            row = [at_level(z, a) * sides + c for c in (1 - b, b) for a in order]
            for t in range(levels):
                for a in (z - t, z + t):
                    row.append(order.index(at_level(z, a)) if 0 <= a < levels else -1)
            plan.append(row)
    info = lax.dynamic_index_in_dim(jnp.asarray(np.array(plan, np.int32)), block, 0, False)

    by_c = amplitudes.transpose(1, 0, 2)

    def hops(pairs, swap):
        return [
            (a * sides + b, c * sides + (sides - 1 - b if swap else b))
            for a, c in pairs
            for b in range(sides)
        ]

    rounds = [(bins, bins)]
    for t in range(1, levels):
        up = [(z, z + 1) for z in range(t - 1, levels - 1)]
        down = [(levels - 1 - a, levels - 1 - c) for a, c in up]
        rounds.append(
            (
                lax.ppermute(rounds[-1][0], "remap", hops(up, False)),
                lax.ppermute(rounds[-1][1], "remap", hops(down, False)),
            )
        )
    places = places_of(orbital_irreps.reshape(blocks, c_rows))
    more = LEFT_MORE * IRREPS
    more_rounds = jnp.maximum(jnp.max(places) - slots + more, 0) // more
    c_at = jnp.maximum(table(places, 0, slots) - 1, 0)
    in_bins = [(0, BINS)]
    split = levels // 2
    stay = hops([(z, z) for z in range(levels)], True)
    def left_term(sent, rows):
        arrived = lax.all_to_all(sent, "remap", split_axis=0, concat_axis=0, tiled=True)
        return left_product(arrived, rows)

    (near,) = route(by_c, c_at, info[:split], in_bins, c_rows, False)
    near = lax.ppermute(near, "remap", stay)
    by_c, rounds[1] = lax.optimization_barrier((by_c, rounds[1]))
    every = jnp.arange(blocks, dtype=jnp.int32)
    (sent,) = route(by_c, c_at, every, [(BINS, LEFT)], c_rows, True)
    (far,) = route(by_c, c_at, info[split:levels], in_bins, c_rows, False)
    (own,) = route(by_c, c_at, info[levels:blocks], in_bins, c_rows, False)
    left_at = own_left(BINS * IRREPS, LEFT * IRREPS)
    sent, left_at, near, rounds[2], code, irr_rows, sym_ab = lax.optimization_barrier(
        (sent, left_at, near, rounds[2], code, irr_rows, sym_ab)
    )
    other = [near, lax.ppermute(far, "remap", stay)]
    total = left_term(sent, left_rows(integrals, code, *left_at))
    rounds[-1], total = lax.optimization_barrier((rounds[-1], total))
    mine = 0
    for t, parts in enumerate(rounds):
        ways = [blocks + 2 * t, blocks + 2 * t + 1]
        if t == 0:
            ways, parts = ways[:1], parts[:1]
        reach = max(row[way] for row in plan for way in ways)
        if t == levels - 1:
            chosen = choose(ways, own, other, info, irr_rows)
            mine = last_product(ways, parts, mine, chosen, info, sym_ab[None, :])
            continue
        mine += bins_product(ways, parts, own, other[: 1 + (reach >= split)], info, irr_rows, sym_ab[None, :])

    def next_round(index, total):
        first = slots + index * more
        c_at = jnp.maximum(table(places, first, more) - 1, 0)
        (sent,) = route(by_c, c_at, every, [(0, LEFT_MORE)], c_rows, True)
        return total + left_term(sent, left_rows(integrals, code, *own_left(first, more)))

    total = lax.fori_loop(0, more_rounds, next_round, total)

    total = total.reshape(blocks, pair_rows, ab_cols)
    ids = jnp.arange(blocks)[:, None, None]
    total = total + jnp.where(ids == block, mine[None, :pair_rows], 0.0)
    total = total + jnp.where(ids == level * sides + 1 - side, mine[None, pair_rows:], 0.0)
    return reduce_to_owners(0.5 * total.reshape(blocks * pair_rows, ab_cols))


def solution(mesh):
    in_specs = (P("remap", None, "rep"), P("remap", "rep", None), P(), P())
    out_specs = P("remap", "rep")
    return jax.shard_map(body, mesh=mesh, in_specs=in_specs, out_specs=out_specs, check_vma=False)
```

```python
import functools

import jax
import jax.numpy as jnp
import numpy as np
from jax import lax
from jax.experimental import pallas as pl
from jax.experimental.pallas import tpu as pltpu
from jax.sharding import PartitionSpec as P

SLABS = 64
IRREPS = 8
BINS = 10
LEFT = 9
LEFT_MORE = 1
VMEM_BYTES = 48 * 1024 * 1024
BYTES_A_US = 3_600_000


def irrep_of(indices, table):
    matches = indices[:, None] == jnp.arange(table.shape[0], dtype=jnp.int32)[None, :]
    return jnp.sum(jnp.where(matches, table[None, :], 0), axis=1)


def sum_kernel(parts_ref, out_ref):
    rows, cols = out_ref.shape
    total = jnp.sum(parts_ref[...], axis=0)
    out_ref[...] = jnp.concatenate(
        [total[:, r * cols : (r + 1) * cols] for r in range(rows)], axis=0
    )


def reduce_to_owners(partial_term):
    remap, rep = lax.axis_size("remap"), lax.axis_size("rep")
    rows, cols = partial_term.shape
    blocks = partial_term.reshape(remap, rows // remap, rep, cols // rep)
    blocks = blocks.transpose(0, 2, 1, 3).reshape(remap * rep, 1, -1)
    arrived = lax.all_to_all(blocks, ("remap", "rep"), split_axis=0, concat_axis=0, tiled=True)
    return pl.pallas_call(
        sum_kernel,
        out_shape=jax.ShapeDtypeStruct((rows // remap, cols // rep), jnp.float32),
        name="sum_parts",
    )(arrived)


def first_plus_one(match):
    c_plus_one = jnp.arange(1, match.shape[1] + 1, dtype=jnp.int32)
    return jnp.sum(jnp.where(match, c_plus_one[None, :, None], 0), axis=1)


def takes(us):
    return pl.CostEstimate(flops=0, bytes_accessed=int(us * BYTES_A_US), transcendentals=0)


def whole(array):
    zeros = (0,) * array.ndim
    return pl.BlockSpec(array.shape, lambda *_: zeros)


def split_lanes(d_cols):
    main = d_cols // 128 * 128
    tail = d_cols - main
    pitch = -(-tail // 16) * 16
    return main, tail, pitch


def pack_kernel(irreps, slab, integrals, out_ref, rows, code_ref, arrived):
    c_rows, d_cols, ab = integrals.shape
    bins = out_ref.shape[0]
    virtual = irreps.shape[0]

    def fetch(c, i):
        return pltpu.make_async_copy(integrals.at[c], rows.at[i], arrived.at[i])

    c_first = lax.axis_index("remap") * c_rows

    def place(c, words):
        h = irreps[c_first + c]
        shift = (h & 3) * 8
        low = h < 4
        g = (jnp.where(low, words[0], words[1]) >> shift) & 255

        @pl.when(g < bins)
        def _():
            fetch(c, g * IRREPS + h).start()

        step = jnp.where(g < bins, jnp.int32(1) << shift, 0)
        return words[0] + jnp.where(low, step, 0), words[1] + jnp.where(low, 0, step)

    words = lax.fori_loop(0, c_rows, place, (jnp.int32(0), jnp.int32(0)), unroll=15)
    counts = [(words[h // 4] >> (h % 4 * 8)) & 255 for h in range(IRREPS)]

    pair = slab[0] * (virtual * virtual // SLABS)
    a_first = pair // virtual
    b_first = pair - a_first * virtual
    lane = lax.broadcasted_iota(jnp.int32, (1, ab), 1)

    def symmetry(k, sym):
        over = (b_first + k >= virtual).astype(jnp.int32)
        value = irreps[a_first + over] ^ irreps[b_first + k - over * virtual]
        return jnp.where(lane == k, value, sym)

    sym = lax.fori_loop(0, ab, symmetry, jnp.zeros((1, ab), jnp.int32), unroll=64)
    d_first = lax.axis_index("rep") * d_cols

    def code_row(d, carry):
        code_ref[pl.ds(d, 1), :] = sym ^ irreps[d_first + d]
        return carry

    lax.fori_loop(0, d_cols, code_row, 0, unroll=75)

    code = code_ref[...].astype(jnp.float32).astype(rows.dtype)

    def one(g, carry):
        for h in range(IRREPS):
            i = g * IRREPS + h

            @pl.when(g < counts[h])
            def _():
                fetch(0, i).wait()

            @pl.when(g >= counts[h])
            def _():
                rows[i] = jnp.zeros((d_cols, ab), rows.dtype)

        total = rows[g * IRREPS]
        for h in range(1, IRREPS):
            total = jnp.where(code == h, rows[g * IRREPS + h], total)
        out_ref[g, pl.ds(0, d_cols)] = total
        return carry

    lax.fori_loop(0, bins, one, 0)


def pack(integrals, irreps, slab):
    _, d_cols, ab = integrals.shape
    padded = -(-d_cols // 16) * 16
    out = jax.ShapeDtypeStruct((BINS, padded, ab), integrals.dtype)
    return pl.pallas_call(
        pack_kernel,
        out_shape=out,
        grid_spec=pltpu.PrefetchScalarGridSpec(
            num_scalar_prefetch=2,
            grid=(1,),
            in_specs=[pl.BlockSpec(memory_space=pl.ANY)],
            out_specs=whole(out),
            scratch_shapes=[
                pltpu.VMEM((BINS * IRREPS, d_cols, ab), integrals.dtype),
                pltpu.VMEM((d_cols, ab), jnp.int32),
                pltpu.SemaphoreType.DMA((BINS * IRREPS,)),
            ],
        ),
        cost_estimate=takes(4),
        compiler_params=pltpu.CompilerParams(vmem_limit_bytes=VMEM_BYTES),
        name="pack_bins",
    )(irreps, slab, integrals)


def route_kernel(firsts, width, c_at, blocks, rows_ref, *outs):
    base = blocks[pl.program_id(0)] * width
    pair_rows, d_cols = rows_ref.shape[1:]
    main, tail, pitch = split_lanes(d_cols)
    for first, out in zip(firsts, outs):

        def one(group, carry):
            tails = []
            for i in range(IRREPS):
                at = c_at[base + (first + group) * IRREPS + i]
                out[0, group, :, pl.ds(i * main, main)] = rows_ref[at, :, pl.ds(0, main)]
                end = rows_ref[at, :, pl.ds(main, tail)].astype(jnp.float32)
                tails += [end, jnp.zeros((pair_rows, pitch - tail), jnp.float32)]
            ends = jnp.concatenate([x for x in tails if x.shape[1]], axis=1)
            out[0, group, :, pl.ds(IRREPS * main, IRREPS * pitch)] = ends.astype(out.dtype)
            return carry

        lax.fori_loop(0, out.shape[1], one, 0)


def route(by_c, c_at, blocks, spans, c_rows, by_block):
    pair_rows, d_cols = by_c.shape[1:]
    steps = blocks.shape[0]
    main, _, pitch = split_lanes(d_cols)
    lanes = IRREPS * (main + pitch)
    at_block = lambda i, c_at, blocks: (blocks[i], 0, 0, 0)
    in_order = lambda i, c_at, blocks: (i, 0, 0, 0)
    return pl.pallas_call(
        functools.partial(route_kernel, [first for first, _ in spans], c_at.shape[1]),
        out_shape=[
            jax.ShapeDtypeStruct((steps, groups, pair_rows, lanes), by_c.dtype)
            for _, groups in spans
        ],
        grid_spec=pltpu.PrefetchScalarGridSpec(
            num_scalar_prefetch=2,
            grid=(steps,),
            in_specs=[
                pl.BlockSpec(
                    (c_rows, pair_rows, d_cols), lambda i, c_at, blocks: (blocks[i], 0, 0)
                )
            ],
            out_specs=[
                pl.BlockSpec((1, groups, pair_rows, lanes), at_block if by_block else in_order)
                for _, groups in spans
            ],
        ),
        cost_estimate=takes(0.1 * steps * sum(groups for _, groups in spans)),
        compiler_params=pltpu.CompilerParams(vmem_limit_bytes=VMEM_BYTES),
        name="route_rows",
    )(c_at.reshape(-1), blocks, by_c)


def chosen_rows(g, lo, size, own, other, level, other_level, irr_d, dtype):
    main, _, pitch = split_lanes(irr_d.shape[1])

    def lane(h):
        return h * main if lo < main else IRREPS * main + h * pitch

    sides = [
        [side[at, g, :, pl.ds(lane(h), size)].astype(jnp.float32) for h in range(IRREPS)]
        for side, at in ((own, level), (other, other_level))
    ]
    irr = irr_d[:, lo : lo + size]
    rows = []
    for s in range(IRREPS):
        for side in sides:
            value = side[s]
            for j in range(1, IRREPS):
                value = jnp.where(irr == j, side[s ^ j], value)
            rows.append(value)
    return jnp.concatenate(rows, axis=0).astype(dtype)


def spans_of(d_cols):
    main, tail, _ = split_lanes(d_cols)
    return [(0, main), (main, tail)] if tail else [(0, main)]


def add_bins(total, bins, own, other, level, other_level, irr_d):
    def one(g, carry):
        sum_ = total[...]
        for lo, size in spans_of(irr_d.shape[1]):
            lhs = chosen_rows(g, lo, size, own, other, level, other_level, irr_d, bins.dtype)
            sum_ += jnp.dot(lhs, bins[g, pl.ds(lo, size)], preferred_element_type=jnp.float32)
        total[...] = sum_
        return carry

    lax.fori_loop(0, bins.shape[0], one, 0)


def pick_symmetry(total, sym, rows):
    picked = jnp.zeros((rows, total.shape[1]), jnp.float32)
    for s in range(IRREPS):
        picked = jnp.where(sym == s, total[pl.ds(s * rows, rows), :], picked)
    return picked


def choose_kernel(places, n_other, info, irr_ref, own, *refs):
    others, out = refs[:n_other], refs[n_other]
    irr_d = irr_ref[...]
    level, first = jnp.maximum(info[places[0]], info[places[1]]), 0
    for other in others:
        last = first + other.shape[0]

        @pl.when((level >= first) & (level < last))
        def _():
            def one(g, carry):
                for lo, size in spans_of(irr_d.shape[1]):
                    out[g, :, pl.ds(lo, size)] = chosen_rows(
                        g, lo, size, own, other, level, level - first, irr_d, out.dtype
                    )
                return carry

            lax.fori_loop(0, out.shape[0], one, 0)

        first = last


def choose(places, own, other, info, irr_d):
    pair_rows, d_cols = irr_d.shape
    tensors = [irr_d, own, *other]
    return pl.pallas_call(
        functools.partial(choose_kernel, places, len(other)),
        out_shape=jax.ShapeDtypeStruct((BINS, IRREPS * 2 * pair_rows, d_cols), own.dtype),
        grid_spec=pltpu.PrefetchScalarGridSpec(
            num_scalar_prefetch=1,
            grid=(1,),
            in_specs=[pl.BlockSpec(memory_space=pltpu.VMEM)] * len(tensors),
            out_specs=pl.BlockSpec(memory_space=pltpu.VMEM),
        ),
        cost_estimate=takes(3),
        compiler_params=pltpu.CompilerParams(vmem_limit_bytes=VMEM_BYTES // 3),
        name="choose_rows",
    )(info, *tensors)


def last_kernel(places, info, sym_ref, before_ref, chosen_ref, up, down, out, total, chosen, bins, arrived):
    rows = pltpu.make_async_copy(chosen_ref, chosen, arrived.at[0])
    rows.start()
    total[...] = jnp.zeros_like(total)
    for place, part in zip(places, (up, down)):

        @pl.when(info[place] >= 0)
        def _():
            copy = pltpu.make_async_copy(part, bins, arrived.at[1])
            copy.start()
            copy.wait()

    rows.wait()

    @pl.when(jnp.maximum(info[places[0]], info[places[1]]) >= 0)
    def _():
        sum_ = jnp.zeros(total.shape, jnp.float32)
        for g in range(bins.shape[0]):
            sum_ += jnp.dot(
                chosen[g], bins[g, pl.ds(0, chosen.shape[2])], preferred_element_type=jnp.float32
            )
        total[...] = sum_

    out[...] = before_ref[...] + pick_symmetry(total, sym_ref[...], out.shape[0])


def last_product(places, parts, before, chosen, info, sym):
    rows, ab = chosen.shape[1], sym.shape[1]
    out = jax.ShapeDtypeStruct((rows // IRREPS, ab), jnp.float32)
    return pl.pallas_call(
        functools.partial(last_kernel, places),
        out_shape=out,
        grid_spec=pltpu.PrefetchScalarGridSpec(
            num_scalar_prefetch=1,
            grid=(1,),
            in_specs=[whole(sym), whole(before)] + [pl.BlockSpec(memory_space=pl.ANY)] * 3,
            out_specs=whole(out),
            scratch_shapes=[
                pltpu.VMEM((rows, ab), jnp.float32),
                pltpu.VMEM(chosen.shape, chosen.dtype),
                pltpu.VMEM(parts[0].shape, parts[0].dtype),
                pltpu.SemaphoreType.DMA((2,)),
            ],
        ),
        cost_estimate=takes(2),
        compiler_params=pltpu.CompilerParams(vmem_limit_bytes=VMEM_BYTES),
        name="last_product",
    )(info, sym, before, chosen, *parts)


def bins_kernel(places, n_other, info, irr_ref, sym_ref, own_ref, *refs):
    other_refs, refs = refs[:n_other], refs[n_other:]
    bins_refs, (out, total, own, other, bins, arrived) = refs[:-6], refs[-6:]
    irr_d, sym = irr_ref[...], sym_ref[...]

    def own_copy(way, level):
        return pltpu.make_async_copy(own_ref.at[level], own.at[way], arrived.at[way, 0])

    def other_copy(way, ref, level):
        return pltpu.make_async_copy(ref.at[level], other.at[way], arrived.at[way, 1])

    def bins_copy(way):
        return pltpu.make_async_copy(bins_refs[way], bins.at[way], arrived.at[way, 2])

    for way, place in enumerate(places):
        level, first = info[place], 0

        @pl.when(level >= 0)
        def _():
            own_copy(way, level).start()
            bins_copy(way).start()

        for ref in other_refs:
            last = first + ref.shape[0]

            @pl.when((level >= first) & (level < last))
            def _():
                other_copy(way, ref, level - first).start()

            first = last

    total[...] = jnp.zeros_like(total)
    for way, place in enumerate(places):

        @pl.when(info[place] >= 0)
        def _():
            own_copy(way, 0).wait()
            other_copy(way, other_refs[0], 0).wait()
            bins_copy(way).wait()
            add_bins(total, bins.at[way], own, other, way, way, irr_d)

    out[...] = pick_symmetry(total, sym, out.shape[0])


def bins_product(places, parts, own, other, info, irr_d, sym):
    pair_rows, ab = irr_d.shape[0], sym.shape[1]
    out = jax.ShapeDtypeStruct((2 * pair_rows, ab), jnp.float32)
    tensors = [own, *other, *parts]
    ways = len(parts)
    return pl.pallas_call(
        functools.partial(bins_kernel, places, len(other)),
        out_shape=out,
        grid_spec=pltpu.PrefetchScalarGridSpec(
            num_scalar_prefetch=1,
            grid=(1,),
            in_specs=[whole(irr_d), whole(sym)]
            + [pl.BlockSpec(memory_space=pl.ANY)] * len(tensors),
            out_specs=whole(out),
            scratch_shapes=[
                pltpu.VMEM((IRREPS * 2 * pair_rows, ab), jnp.float32),
                pltpu.VMEM((ways, *own.shape[1:]), own.dtype),
                pltpu.VMEM((ways, *own.shape[1:]), own.dtype),
                pltpu.VMEM((ways, *parts[0].shape), parts[0].dtype),
                pltpu.SemaphoreType.DMA((ways, 3)),
            ],
        ),
        cost_estimate=takes(3),
        compiler_params=pltpu.CompilerParams(vmem_limit_bytes=VMEM_BYTES),
        name="bins_product",
    )(info, irr_d, sym, *tensors)


def left_rows_kernel(slots, irreps, code_ref, integrals, out_ref, rows, arrived):
    group = pl.program_id(0)
    d_cols, ab = code_ref.shape
    main, tail, pitch = split_lanes(d_cols)

    def fetch(i):
        c = jnp.maximum(slots[i] - 1, 0)
        return pltpu.make_async_copy(integrals.at[c], rows.at[i], arrived.at[i])

    def start(i, carry):
        fetch(i).start()
        return carry

    @pl.when(group == 0)
    def _():
        lax.fori_loop(0, rows.shape[0], start, 0)

    code = code_ref[...]
    for h in range(IRREPS):
        i = group * IRREPS + h
        fetch(i).wait()
        irrep = jnp.where(slots[i] > 0, irreps[i], IRREPS)
        row = jnp.where(code == irrep, rows[i].astype(jnp.float32), 0.0)
        out_ref[0, pl.ds(h * main, main)] = row[:main].astype(out_ref.dtype)
        if tail:
            end = row[main:]
            if pitch > tail:
                end = jnp.concatenate([end, jnp.zeros((pitch - tail, ab), jnp.float32)], axis=0)
            out_ref[0, pl.ds(IRREPS * main + h * pitch, pitch)] = end.astype(out_ref.dtype)


def left_rows(integrals, code, slots, irreps):
    d_cols, ab = code.shape
    count = slots.shape[0]
    main, _, pitch = split_lanes(d_cols)
    depth = IRREPS * (main + pitch)
    return pl.pallas_call(
        left_rows_kernel,
        out_shape=jax.ShapeDtypeStruct((count // IRREPS, depth, ab), integrals.dtype),
        grid_spec=pltpu.PrefetchScalarGridSpec(
            num_scalar_prefetch=2,
            grid=(count // IRREPS,),
            in_specs=[whole(code), pl.BlockSpec(memory_space=pl.ANY)],
            out_specs=pl.BlockSpec((1, depth, ab), lambda i, *_: (i, 0, 0)),
            scratch_shapes=[
                pltpu.VMEM((count, d_cols, ab), integrals.dtype),
                pltpu.SemaphoreType.DMA((count,)),
            ],
        ),
        cost_estimate=takes(5),
        compiler_params=pltpu.CompilerParams(vmem_limit_bytes=VMEM_BYTES),
        name="left_rows",
    )(slots, irreps, code, integrals)


def left_kernel(amp_ref, row_ref, out_ref, amps, rows, amps_here, rows_here):
    sources, groups, pair_rows, depth = amp_ref.shape
    edges = [groups * i // 3 for i in range(4)]
    parts = [(lo, hi - lo) for lo, hi in zip(edges, edges[1:]) if hi > lo]
    parts = [(at, pl.ds(lo, size), lo, size) for at, (lo, size) in enumerate(parts)]
    copies = []
    for at, span, lo, size in parts:
        copies.append(
            [
                pltpu.make_async_copy(
                    amp_ref.at[source, span], amps.at[source, span], amps_here.at[at, source]
                )
                for source in range(sources)
            ]
            + [
                pltpu.make_async_copy(row_ref.at[group], rows.at[group], rows_here.at[group])
                for group in range(lo, lo + size)
            ]
        )
    for part in copies:
        for copy in part:
            copy.start()
    total = jnp.zeros(out_ref.shape, jnp.float32)
    for part, (_, _, lo, size) in zip(copies, parts):
        for copy in part:
            copy.wait()
        for group in range(lo, lo + size):
            lhs = amps[:, group].astype(jnp.float32).reshape(sources * pair_rows, depth)
            total += jnp.dot(
                lhs.astype(rows.dtype), rows[group], preferred_element_type=jnp.float32
            )
    out_ref[...] = total


def left_product(amps, rows):
    sources, groups, pair_rows, depth = amps.shape
    ab = rows.shape[2]
    return pl.pallas_call(
        left_kernel,
        out_shape=jax.ShapeDtypeStruct((sources * pair_rows, ab), jnp.float32),
        in_specs=[pl.BlockSpec(memory_space=pl.ANY)] * 2,
        out_specs=pl.BlockSpec(memory_space=pltpu.VMEM),
        scratch_shapes=[
            pltpu.VMEM(amps.shape, amps.dtype),
            pltpu.VMEM(rows.shape, rows.dtype),
            pltpu.SemaphoreType.DMA((3, sources)),
            pltpu.SemaphoreType.DMA((groups,)),
        ],
        cost_estimate=takes(5),
        compiler_params=pltpu.CompilerParams(vmem_limit_bytes=VMEM_BYTES),
        name="left_product",
    )(amps, rows)


def body(amplitudes, integrals, orbital_irreps, slab_index):
    c_rows, d_cols, ab_cols = integrals.shape
    pair_rows = amplitudes.shape[0]
    virtual = orbital_irreps.shape[0]
    blocks = lax.axis_size("remap")
    sides = 2
    levels = blocks // sides
    assert levels >= 2 and blocks == levels * sides
    block = lax.axis_index("remap")
    level, side = block // sides, block % sides
    slots = (BINS + LEFT) * IRREPS

    bins = pack(integrals, orbital_irreps, slab_index)
    amplitudes, orbital_irreps, bins = lax.optimization_barrier((amplitudes, orbital_irreps, bins))

    earlier = jnp.arange(c_rows)[:, None] < jnp.arange(c_rows)[None, :]

    def places_of(irr):
        alike = (irr[:, :, None] == irr[:, None, :]) & earlier[None]
        rank = jnp.sum(alike.astype(jnp.int32), axis=1)
        over = rank >= BINS
        left_rank = jnp.sum((over[:, :, None] & earlier[None]).astype(jnp.int32), axis=1)
        return jnp.where(over, BINS * IRREPS + left_rank, rank * IRREPS + irr)

    def table(places, first, count):
        wanted = first + jnp.arange(count, dtype=jnp.int32)
        return first_plus_one(places[:, :, None] == wanted[None, None, :])

    own_irr = lax.dynamic_slice_in_dim(orbital_irreps, block * c_rows, c_rows, 0)
    own_places = places_of(own_irr[None])

    def own_left(first, count):
        match = own_places[0][:, None] == first + jnp.arange(count, dtype=jnp.int32)[None, :]
        irreps = jnp.sum(jnp.where(match, own_irr[:, None], 0), axis=0)
        return first_plus_one(match[None])[0], irreps

    irr_d = lax.dynamic_slice_in_dim(orbital_irreps, lax.axis_index("rep") * d_cols, d_cols, 0)
    stride = virtual * virtual // SLABS
    pair_ab = slab_index[0] * stride + jnp.arange(ab_cols, dtype=jnp.int32)
    sym_ab = jnp.bitwise_xor(
        irrep_of(pair_ab // virtual, orbital_irreps), irrep_of(pair_ab % virtual, orbital_irreps)
    )
    code = jnp.bitwise_xor(irr_d[:, None], sym_ab[None, :])
    irr_rows = jnp.broadcast_to(irr_d[None, :], (pair_rows, d_cols))

    order = [1, 0] + list(range(2, levels))

    def at_level(z, a):
        return a if z < levels // 2 else levels - 1 - a

    plan = []
    for z in range(levels):
        for b in range(sides):
            row = [at_level(z, a) * sides + c for c in (1 - b, b) for a in order]
            for t in range(levels):
                for a in (z - t, z + t):
                    row.append(order.index(at_level(z, a)) if 0 <= a < levels else -1)
            plan.append(row)
    info = lax.dynamic_index_in_dim(jnp.asarray(np.array(plan, np.int32)), block, 0, False)

    by_c = amplitudes.transpose(1, 0, 2)

    def hops(pairs, swap):
        return [
            (a * sides + b, c * sides + (sides - 1 - b if swap else b))
            for a, c in pairs
            for b in range(sides)
        ]

    rounds = [(bins, bins)]
    for t in range(1, levels):
        up = [(z, z + 1) for z in range(t - 1, levels - 1)]
        down = [(levels - 1 - a, levels - 1 - c) for a, c in up]
        rounds.append(
            (
                lax.ppermute(rounds[-1][0], "remap", hops(up, False)),
                lax.ppermute(rounds[-1][1], "remap", hops(down, False)),
            )
        )
    places = places_of(orbital_irreps.reshape(blocks, c_rows))
    more = LEFT_MORE * IRREPS
    more_rounds = jnp.maximum(jnp.max(places) - slots + more, 0) // more
    c_at = jnp.maximum(table(places, 0, slots) - 1, 0)
    in_bins = [(0, BINS)]
    split = levels // 2
    stay = hops([(z, z) for z in range(levels)], True)
    def left_term(sent, rows):
        arrived = lax.all_to_all(sent, "remap", split_axis=0, concat_axis=0, tiled=True)
        return left_product(arrived, rows)

    (near,) = route(by_c, c_at, info[:split], in_bins, c_rows, False)
    near = lax.ppermute(near, "remap", stay)
    by_c, rounds[1] = lax.optimization_barrier((by_c, rounds[1]))
    every = jnp.arange(blocks, dtype=jnp.int32)
    (sent,) = route(by_c, c_at, every, [(BINS, LEFT)], c_rows, True)
    (far,) = route(by_c, c_at, info[split:levels], in_bins, c_rows, False)
    (own,) = route(by_c, c_at, info[levels:blocks], in_bins, c_rows, False)
    left_at = own_left(BINS * IRREPS, LEFT * IRREPS)
    sent, left_at, near, rounds[2], code, irr_rows, sym_ab = lax.optimization_barrier(
        (sent, left_at, near, rounds[2], code, irr_rows, sym_ab)
    )
    other = [near, lax.ppermute(far, "remap", stay)]
    total = left_term(sent, left_rows(integrals, code, *left_at))
    rounds[-1], total = lax.optimization_barrier((rounds[-1], total))
    mine = 0
    for t, parts in enumerate(rounds):
        ways = [blocks + 2 * t, blocks + 2 * t + 1]
        if t == 0:
            ways, parts = ways[:1], parts[:1]
        reach = max(row[way] for row in plan for way in ways)
        if t == levels - 1:
            chosen = choose(ways, own, other, info, irr_rows)
            mine = last_product(ways, parts, mine, chosen, info, sym_ab[None, :])
            continue
        mine += bins_product(ways, parts, own, other[: 1 + (reach >= split)], info, irr_rows, sym_ab[None, :])

    def next_round(index, total):
        first = slots + index * more
        c_at = jnp.maximum(table(places, first, more) - 1, 0)
        (sent,) = route(by_c, c_at, every, [(0, LEFT_MORE)], c_rows, True)
        return total + left_term(sent, left_rows(integrals, code, *own_left(first, more)))

    total = lax.fori_loop(0, more_rounds, next_round, total)

    total = total.reshape(blocks, pair_rows, ab_cols)
    ids = jnp.arange(blocks)[:, None, None]
    total = total + jnp.where(ids == block, mine[None, :pair_rows], 0.0)
    total = total + jnp.where(ids == level * sides + 1 - side, mine[None, pair_rows:], 0.0)
    return reduce_to_owners(0.5 * total.reshape(blocks * pair_rows, ab_cols))


def solution(mesh):
    in_specs = (P("remap", None, "rep"), P("remap", "rep", None), P(), P())
    out_specs = P("remap", "rep")
    return jax.shard_map(body, mesh=mesh, in_specs=in_specs, out_specs=out_specs, check_vma=False)
```

```python
import functools

import jax
import jax.numpy as jnp
import numpy as np
from jax import lax
from jax.experimental import pallas as pl
from jax.experimental.pallas import tpu as pltpu
from jax.sharding import PartitionSpec as P

SLABS = 64
IRREPS = 8
BINS = 10
LEFT = 9
LEFT_MORE = 1
VMEM_BYTES = 48 * 1024 * 1024
BYTES_A_US = 3_600_000


def irrep_of(indices, table):
    matches = indices[:, None] == jnp.arange(table.shape[0], dtype=jnp.int32)[None, :]
    return jnp.sum(jnp.where(matches, table[None, :], 0), axis=1)


def sum_kernel(parts_ref, out_ref):
    rows, cols = out_ref.shape
    total = jnp.sum(parts_ref[...], axis=0)
    out_ref[...] = jnp.concatenate(
        [total[:, r * cols : (r + 1) * cols] for r in range(rows)], axis=0
    )


def reduce_to_owners(partial_term):
    remap, rep = lax.axis_size("remap"), lax.axis_size("rep")
    rows, cols = partial_term.shape
    blocks = partial_term.reshape(remap, rows // remap, rep, cols // rep)
    blocks = blocks.transpose(0, 2, 1, 3).reshape(remap * rep, 1, -1)
    arrived = lax.all_to_all(blocks, ("remap", "rep"), split_axis=0, concat_axis=0, tiled=True)
    return pl.pallas_call(
        sum_kernel,
        out_shape=jax.ShapeDtypeStruct((rows // remap, cols // rep), jnp.float32),
        name="sum_parts",
    )(arrived)


def first_plus_one(match):
    c_plus_one = jnp.arange(1, match.shape[1] + 1, dtype=jnp.int32)
    return jnp.sum(jnp.where(match, c_plus_one[None, :, None], 0), axis=1)


def takes(us):
    return pl.CostEstimate(flops=0, bytes_accessed=int(us * BYTES_A_US), transcendentals=0)


def whole(array):
    zeros = (0,) * array.ndim
    return pl.BlockSpec(array.shape, lambda *_: zeros)


def split_lanes(d_cols):
    main = d_cols // 128 * 128
    tail = d_cols - main
    pitch = -(-tail // 16) * 16
    return main, tail, pitch


def pack_kernel(irreps, slab, integrals, out_ref, rows, code_ref, arrived):
    c_rows, d_cols, ab = integrals.shape
    bins = out_ref.shape[0]
    virtual = irreps.shape[0]

    def fetch(c, i):
        return pltpu.make_async_copy(integrals.at[c], rows.at[i], arrived.at[i])

    c_first = lax.axis_index("remap") * c_rows

    def place(c, words):
        h = irreps[c_first + c]
        shift = (h & 3) * 8
        low = h < 4
        g = (jnp.where(low, words[0], words[1]) >> shift) & 255

        @pl.when(g < bins)
        def _():
            fetch(c, g * IRREPS + h).start()

        step = jnp.where(g < bins, jnp.int32(1) << shift, 0)
        return words[0] + jnp.where(low, step, 0), words[1] + jnp.where(low, 0, step)

    words = lax.fori_loop(0, c_rows, place, (jnp.int32(0), jnp.int32(0)), unroll=15)
    counts = [(words[h // 4] >> (h % 4 * 8)) & 255 for h in range(IRREPS)]

    pair = slab[0] * (virtual * virtual // SLABS)
    a_first = pair // virtual
    b_first = pair - a_first * virtual
    lane = lax.broadcasted_iota(jnp.int32, (1, ab), 1)

    def symmetry(k, sym):
        over = (b_first + k >= virtual).astype(jnp.int32)
        value = irreps[a_first + over] ^ irreps[b_first + k - over * virtual]
        return jnp.where(lane == k, value, sym)

    sym = lax.fori_loop(0, ab, symmetry, jnp.zeros((1, ab), jnp.int32), unroll=64)
    d_first = lax.axis_index("rep") * d_cols

    def code_row(d, carry):
        code_ref[pl.ds(d, 1), :] = sym ^ irreps[d_first + d]
        return carry

    lax.fori_loop(0, d_cols, code_row, 0, unroll=75)

    code = code_ref[...].astype(jnp.float32).astype(rows.dtype)

    def one(g, carry):
        for h in range(IRREPS):
            i = g * IRREPS + h

            @pl.when(g < counts[h])
            def _():
                fetch(0, i).wait()

            @pl.when(g >= counts[h])
            def _():
                rows[i] = jnp.zeros((d_cols, ab), rows.dtype)

        total = rows[g * IRREPS]
        for h in range(1, IRREPS):
            total = jnp.where(code == h, rows[g * IRREPS + h], total)
        out_ref[g, pl.ds(0, d_cols)] = total
        return carry

    lax.fori_loop(0, bins, one, 0, unroll=2)


def pack(integrals, irreps, slab):
    _, d_cols, ab = integrals.shape
    padded = -(-d_cols // 16) * 16
    out = jax.ShapeDtypeStruct((BINS, padded, ab), integrals.dtype)
    return pl.pallas_call(
        pack_kernel,
        out_shape=out,
        grid_spec=pltpu.PrefetchScalarGridSpec(
            num_scalar_prefetch=2,
            grid=(1,),
            in_specs=[pl.BlockSpec(memory_space=pl.ANY)],
            out_specs=whole(out),
            scratch_shapes=[
                pltpu.VMEM((BINS * IRREPS, d_cols, ab), integrals.dtype),
                pltpu.VMEM((d_cols, ab), jnp.int32),
                pltpu.SemaphoreType.DMA((BINS * IRREPS,)),
            ],
        ),
        cost_estimate=takes(4),
        compiler_params=pltpu.CompilerParams(vmem_limit_bytes=VMEM_BYTES),
        name="pack_bins",
    )(irreps, slab, integrals)


def route_kernel(firsts, width, c_at, blocks, rows_ref, *outs):
    base = blocks[pl.program_id(0)] * width
    pair_rows, d_cols = rows_ref.shape[1:]
    main, tail, pitch = split_lanes(d_cols)
    for first, out in zip(firsts, outs):

        def one(group, carry):
            tails = []
            for i in range(IRREPS):
                at = c_at[base + (first + group) * IRREPS + i]
                out[0, group, :, pl.ds(i * main, main)] = rows_ref[at, :, pl.ds(0, main)]
                end = rows_ref[at, :, pl.ds(main, tail)].astype(jnp.float32)
                tails += [end, jnp.zeros((pair_rows, pitch - tail), jnp.float32)]
            ends = jnp.concatenate([x for x in tails if x.shape[1]], axis=1)
            out[0, group, :, pl.ds(IRREPS * main, IRREPS * pitch)] = ends.astype(out.dtype)
            return carry

        lax.fori_loop(0, out.shape[1], one, 0)


def route(by_c, c_at, blocks, spans, c_rows, by_block):
    pair_rows, d_cols = by_c.shape[1:]
    steps = blocks.shape[0]
    main, _, pitch = split_lanes(d_cols)
    lanes = IRREPS * (main + pitch)
    at_block = lambda i, c_at, blocks: (blocks[i], 0, 0, 0)
    in_order = lambda i, c_at, blocks: (i, 0, 0, 0)
    return pl.pallas_call(
        functools.partial(route_kernel, [first for first, _ in spans], c_at.shape[1]),
        out_shape=[
            jax.ShapeDtypeStruct((steps, groups, pair_rows, lanes), by_c.dtype)
            for _, groups in spans
        ],
        grid_spec=pltpu.PrefetchScalarGridSpec(
            num_scalar_prefetch=2,
            grid=(steps,),
            in_specs=[
                pl.BlockSpec(
                    (c_rows, pair_rows, d_cols), lambda i, c_at, blocks: (blocks[i], 0, 0)
                )
            ],
            out_specs=[
                pl.BlockSpec((1, groups, pair_rows, lanes), at_block if by_block else in_order)
                for _, groups in spans
            ],
        ),
        cost_estimate=takes(0.1 * steps * sum(groups for _, groups in spans)),
        compiler_params=pltpu.CompilerParams(vmem_limit_bytes=VMEM_BYTES),
        name="route_rows",
    )(c_at.reshape(-1), blocks, by_c)


def chosen_rows(g, lo, size, own, other, level, other_level, irr_d, dtype):
    main, _, pitch = split_lanes(irr_d.shape[1])

    def lane(h):
        return h * main if lo < main else IRREPS * main + h * pitch

    sides = [
        [side[at, g, :, pl.ds(lane(h), size)].astype(jnp.float32) for h in range(IRREPS)]
        for side, at in ((own, level), (other, other_level))
    ]
    irr = irr_d[:, lo : lo + size]
    rows = []
    for s in range(IRREPS):
        for side in sides:
            value = side[s]
            for j in range(1, IRREPS):
                value = jnp.where(irr == j, side[s ^ j], value)
            rows.append(value)
    return jnp.concatenate(rows, axis=0).astype(dtype)


def spans_of(d_cols):
    main, tail, _ = split_lanes(d_cols)
    return [(0, main), (main, tail)] if tail else [(0, main)]


def add_bins(total, bins, own, other, level, other_level, irr_d):
    def one(g, carry):
        sum_ = total[...]
        for lo, size in spans_of(irr_d.shape[1]):
            lhs = chosen_rows(g, lo, size, own, other, level, other_level, irr_d, bins.dtype)
            sum_ += jnp.dot(lhs, bins[g, pl.ds(lo, size)], preferred_element_type=jnp.float32)
        total[...] = sum_
        return carry

    lax.fori_loop(0, bins.shape[0], one, 0)


def pick_symmetry(total, sym, rows):
    picked = jnp.zeros((rows, total.shape[1]), jnp.float32)
    for s in range(IRREPS):
        picked = jnp.where(sym == s, total[pl.ds(s * rows, rows), :], picked)
    return picked


def choose_kernel(places, n_other, info, irr_ref, own, *refs):
    others, out = refs[:n_other], refs[n_other]
    irr_d = irr_ref[...]
    level, first = jnp.maximum(info[places[0]], info[places[1]]), 0
    for other in others:
        last = first + other.shape[0]

        @pl.when((level >= first) & (level < last))
        def _():
            def one(g, carry):
                for lo, size in spans_of(irr_d.shape[1]):
                    out[g, :, pl.ds(lo, size)] = chosen_rows(
                        g, lo, size, own, other, level, level - first, irr_d, out.dtype
                    )
                return carry

            lax.fori_loop(0, out.shape[0], one, 0)

        first = last


def choose(places, own, other, info, irr_d):
    pair_rows, d_cols = irr_d.shape
    tensors = [irr_d, own, *other]
    return pl.pallas_call(
        functools.partial(choose_kernel, places, len(other)),
        out_shape=jax.ShapeDtypeStruct((BINS, IRREPS * 2 * pair_rows, d_cols), own.dtype),
        grid_spec=pltpu.PrefetchScalarGridSpec(
            num_scalar_prefetch=1,
            grid=(1,),
            in_specs=[pl.BlockSpec(memory_space=pltpu.VMEM)] * len(tensors),
            out_specs=pl.BlockSpec(memory_space=pltpu.VMEM),
        ),
        cost_estimate=takes(3),
        compiler_params=pltpu.CompilerParams(vmem_limit_bytes=VMEM_BYTES // 3),
        name="choose_rows",
    )(info, *tensors)


def last_kernel(places, info, sym_ref, before_ref, chosen_ref, up, down, out, total, chosen, bins, arrived):
    rows = pltpu.make_async_copy(chosen_ref, chosen, arrived.at[0])
    rows.start()
    total[...] = jnp.zeros_like(total)
    for place, part in zip(places, (up, down)):

        @pl.when(info[place] >= 0)
        def _():
            copy = pltpu.make_async_copy(part, bins, arrived.at[1])
            copy.start()
            copy.wait()

    rows.wait()

    @pl.when(jnp.maximum(info[places[0]], info[places[1]]) >= 0)
    def _():
        sum_ = jnp.zeros(total.shape, jnp.float32)
        for g in range(bins.shape[0]):
            sum_ += jnp.dot(
                chosen[g], bins[g, pl.ds(0, chosen.shape[2])], preferred_element_type=jnp.float32
            )
        total[...] = sum_

    out[...] = before_ref[...] + pick_symmetry(total, sym_ref[...], out.shape[0])


def last_product(places, parts, before, chosen, info, sym):
    rows, ab = chosen.shape[1], sym.shape[1]
    out = jax.ShapeDtypeStruct((rows // IRREPS, ab), jnp.float32)
    return pl.pallas_call(
        functools.partial(last_kernel, places),
        out_shape=out,
        grid_spec=pltpu.PrefetchScalarGridSpec(
            num_scalar_prefetch=1,
            grid=(1,),
            in_specs=[whole(sym), whole(before)] + [pl.BlockSpec(memory_space=pl.ANY)] * 3,
            out_specs=whole(out),
            scratch_shapes=[
                pltpu.VMEM((rows, ab), jnp.float32),
                pltpu.VMEM(chosen.shape, chosen.dtype),
                pltpu.VMEM(parts[0].shape, parts[0].dtype),
                pltpu.SemaphoreType.DMA((2,)),
            ],
        ),
        cost_estimate=takes(2),
        compiler_params=pltpu.CompilerParams(vmem_limit_bytes=VMEM_BYTES),
        name="last_product",
    )(info, sym, before, chosen, *parts)


def bins_kernel(places, n_other, info, irr_ref, sym_ref, own_ref, *refs):
    other_refs, refs = refs[:n_other], refs[n_other:]
    bins_refs, (out, total, own, other, bins, arrived) = refs[:-6], refs[-6:]
    irr_d, sym = irr_ref[...], sym_ref[...]

    def own_copy(way, level):
        return pltpu.make_async_copy(own_ref.at[level], own.at[way], arrived.at[way, 0])

    def other_copy(way, ref, level):
        return pltpu.make_async_copy(ref.at[level], other.at[way], arrived.at[way, 1])

    def bins_copy(way):
        return pltpu.make_async_copy(bins_refs[way], bins.at[way], arrived.at[way, 2])

    for way, place in enumerate(places):
        level, first = info[place], 0

        @pl.when(level >= 0)
        def _():
            own_copy(way, level).start()
            bins_copy(way).start()

        for ref in other_refs:
            last = first + ref.shape[0]

            @pl.when((level >= first) & (level < last))
            def _():
                other_copy(way, ref, level - first).start()

            first = last

    total[...] = jnp.zeros_like(total)
    for way, place in enumerate(places):

        @pl.when(info[place] >= 0)
        def _():
            own_copy(way, 0).wait()
            other_copy(way, other_refs[0], 0).wait()
            bins_copy(way).wait()
            add_bins(total, bins.at[way], own, other, way, way, irr_d)

    out[...] = pick_symmetry(total, sym, out.shape[0])


def bins_product(places, parts, own, other, info, irr_d, sym):
    pair_rows, ab = irr_d.shape[0], sym.shape[1]
    out = jax.ShapeDtypeStruct((2 * pair_rows, ab), jnp.float32)
    tensors = [own, *other, *parts]
    ways = len(parts)
    return pl.pallas_call(
        functools.partial(bins_kernel, places, len(other)),
        out_shape=out,
        grid_spec=pltpu.PrefetchScalarGridSpec(
            num_scalar_prefetch=1,
            grid=(1,),
            in_specs=[whole(irr_d), whole(sym)]
            + [pl.BlockSpec(memory_space=pl.ANY)] * len(tensors),
            out_specs=whole(out),
            scratch_shapes=[
                pltpu.VMEM((IRREPS * 2 * pair_rows, ab), jnp.float32),
                pltpu.VMEM((ways, *own.shape[1:]), own.dtype),
                pltpu.VMEM((ways, *own.shape[1:]), own.dtype),
                pltpu.VMEM((ways, *parts[0].shape), parts[0].dtype),
                pltpu.SemaphoreType.DMA((ways, 3)),
            ],
        ),
        cost_estimate=takes(3),
        compiler_params=pltpu.CompilerParams(vmem_limit_bytes=VMEM_BYTES),
        name="bins_product",
    )(info, irr_d, sym, *tensors)


def left_rows_kernel(slots, irreps, code_ref, integrals, out_ref, rows, arrived):
    group = pl.program_id(0)
    d_cols, ab = code_ref.shape
    main, tail, pitch = split_lanes(d_cols)

    def fetch(i):
        c = jnp.maximum(slots[i] - 1, 0)
        return pltpu.make_async_copy(integrals.at[c], rows.at[i], arrived.at[i])

    def start(i, carry):
        fetch(i).start()
        return carry

    @pl.when(group == 0)
    def _():
        lax.fori_loop(0, rows.shape[0], start, 0)

    code = code_ref[...]
    for h in range(IRREPS):
        i = group * IRREPS + h
        fetch(i).wait()
        irrep = jnp.where(slots[i] > 0, irreps[i], IRREPS)
        row = jnp.where(code == irrep, rows[i].astype(jnp.float32), 0.0)
        out_ref[0, pl.ds(h * main, main)] = row[:main].astype(out_ref.dtype)
        if tail:
            end = row[main:]
            if pitch > tail:
                end = jnp.concatenate([end, jnp.zeros((pitch - tail, ab), jnp.float32)], axis=0)
            out_ref[0, pl.ds(IRREPS * main + h * pitch, pitch)] = end.astype(out_ref.dtype)


def left_rows(integrals, code, slots, irreps):
    d_cols, ab = code.shape
    count = slots.shape[0]
    main, _, pitch = split_lanes(d_cols)
    depth = IRREPS * (main + pitch)
    return pl.pallas_call(
        left_rows_kernel,
        out_shape=jax.ShapeDtypeStruct((count // IRREPS, depth, ab), integrals.dtype),
        grid_spec=pltpu.PrefetchScalarGridSpec(
            num_scalar_prefetch=2,
            grid=(count // IRREPS,),
            in_specs=[whole(code), pl.BlockSpec(memory_space=pl.ANY)],
            out_specs=pl.BlockSpec((1, depth, ab), lambda i, *_: (i, 0, 0)),
            scratch_shapes=[
                pltpu.VMEM((count, d_cols, ab), integrals.dtype),
                pltpu.SemaphoreType.DMA((count,)),
            ],
        ),
        cost_estimate=takes(5),
        compiler_params=pltpu.CompilerParams(vmem_limit_bytes=VMEM_BYTES),
        name="left_rows",
    )(slots, irreps, code, integrals)


def left_kernel(amp_ref, row_ref, out_ref, amps, rows, amps_here, rows_here):
    sources, groups, pair_rows, depth = amp_ref.shape
    edges = [groups * i // 3 for i in range(4)]
    parts = [(lo, hi - lo) for lo, hi in zip(edges, edges[1:]) if hi > lo]
    parts = [(at, pl.ds(lo, size), lo, size) for at, (lo, size) in enumerate(parts)]
    copies = []
    for at, span, lo, size in parts:
        copies.append(
            [
                pltpu.make_async_copy(
                    amp_ref.at[source, span], amps.at[source, span], amps_here.at[at, source]
                )
                for source in range(sources)
            ]
            + [
                pltpu.make_async_copy(row_ref.at[group], rows.at[group], rows_here.at[group])
                for group in range(lo, lo + size)
            ]
        )
    for part in copies:
        for copy in part:
            copy.start()
    total = jnp.zeros(out_ref.shape, jnp.float32)
    for part, (_, _, lo, size) in zip(copies, parts):
        for copy in part:
            copy.wait()
        for group in range(lo, lo + size):
            lhs = amps[:, group].astype(jnp.float32).reshape(sources * pair_rows, depth)
            total += jnp.dot(
                lhs.astype(rows.dtype), rows[group], preferred_element_type=jnp.float32
            )
    out_ref[...] = total


def left_product(amps, rows):
    sources, groups, pair_rows, depth = amps.shape
    ab = rows.shape[2]
    return pl.pallas_call(
        left_kernel,
        out_shape=jax.ShapeDtypeStruct((sources * pair_rows, ab), jnp.float32),
        in_specs=[pl.BlockSpec(memory_space=pl.ANY)] * 2,
        out_specs=pl.BlockSpec(memory_space=pltpu.VMEM),
        scratch_shapes=[
            pltpu.VMEM(amps.shape, amps.dtype),
            pltpu.VMEM(rows.shape, rows.dtype),
            pltpu.SemaphoreType.DMA((3, sources)),
            pltpu.SemaphoreType.DMA((groups,)),
        ],
        cost_estimate=takes(5),
        compiler_params=pltpu.CompilerParams(vmem_limit_bytes=VMEM_BYTES),
        name="left_product",
    )(amps, rows)


def body(amplitudes, integrals, orbital_irreps, slab_index):
    c_rows, d_cols, ab_cols = integrals.shape
    pair_rows = amplitudes.shape[0]
    virtual = orbital_irreps.shape[0]
    blocks = lax.axis_size("remap")
    sides = 2
    levels = blocks // sides
    assert levels >= 2 and blocks == levels * sides
    block = lax.axis_index("remap")
    level, side = block // sides, block % sides
    slots = (BINS + LEFT) * IRREPS

    bins = pack(integrals, orbital_irreps, slab_index)
    amplitudes, orbital_irreps, bins = lax.optimization_barrier((amplitudes, orbital_irreps, bins))

    earlier = jnp.arange(c_rows)[:, None] < jnp.arange(c_rows)[None, :]

    def places_of(irr):
        alike = (irr[:, :, None] == irr[:, None, :]) & earlier[None]
        rank = jnp.sum(alike.astype(jnp.int32), axis=1)
        over = rank >= BINS
        left_rank = jnp.sum((over[:, :, None] & earlier[None]).astype(jnp.int32), axis=1)
        return jnp.where(over, BINS * IRREPS + left_rank, rank * IRREPS + irr)

    def table(places, first, count):
        wanted = first + jnp.arange(count, dtype=jnp.int32)
        return first_plus_one(places[:, :, None] == wanted[None, None, :])

    own_irr = lax.dynamic_slice_in_dim(orbital_irreps, block * c_rows, c_rows, 0)
    own_places = places_of(own_irr[None])

    def own_left(first, count):
        match = own_places[0][:, None] == first + jnp.arange(count, dtype=jnp.int32)[None, :]
        irreps = jnp.sum(jnp.where(match, own_irr[:, None], 0), axis=0)
        return first_plus_one(match[None])[0], irreps

    irr_d = lax.dynamic_slice_in_dim(orbital_irreps, lax.axis_index("rep") * d_cols, d_cols, 0)
    stride = virtual * virtual // SLABS
    pair_ab = slab_index[0] * stride + jnp.arange(ab_cols, dtype=jnp.int32)
    sym_ab = jnp.bitwise_xor(
        irrep_of(pair_ab // virtual, orbital_irreps), irrep_of(pair_ab % virtual, orbital_irreps)
    )
    code = jnp.bitwise_xor(irr_d[:, None], sym_ab[None, :])
    irr_rows = jnp.broadcast_to(irr_d[None, :], (pair_rows, d_cols))

    order = [1, 0] + list(range(2, levels))

    def at_level(z, a):
        return a if z < levels // 2 else levels - 1 - a

    plan = []
    for z in range(levels):
        for b in range(sides):
            row = [at_level(z, a) * sides + c for c in (1 - b, b) for a in order]
            for t in range(levels):
                for a in (z - t, z + t):
                    row.append(order.index(at_level(z, a)) if 0 <= a < levels else -1)
            plan.append(row)
    info = lax.dynamic_index_in_dim(jnp.asarray(np.array(plan, np.int32)), block, 0, False)

    by_c = amplitudes.transpose(1, 0, 2)

    def hops(pairs, swap):
        return [
            (a * sides + b, c * sides + (sides - 1 - b if swap else b))
            for a, c in pairs
            for b in range(sides)
        ]

    rounds = [(bins, bins)]
    for t in range(1, levels):
        up = [(z, z + 1) for z in range(t - 1, levels - 1)]
        down = [(levels - 1 - a, levels - 1 - c) for a, c in up]
        rounds.append(
            (
                lax.ppermute(rounds[-1][0], "remap", hops(up, False)),
                lax.ppermute(rounds[-1][1], "remap", hops(down, False)),
            )
        )
    places = places_of(orbital_irreps.reshape(blocks, c_rows))
    more = LEFT_MORE * IRREPS
    more_rounds = jnp.maximum(jnp.max(places) - slots + more, 0) // more
    c_at = jnp.maximum(table(places, 0, slots) - 1, 0)
    in_bins = [(0, BINS)]
    split = levels // 2
    stay = hops([(z, z) for z in range(levels)], True)
    def left_term(sent, rows):
        arrived = lax.all_to_all(sent, "remap", split_axis=0, concat_axis=0, tiled=True)
        return left_product(arrived, rows)

    (near,) = route(by_c, c_at, info[:split], in_bins, c_rows, False)
    near = lax.ppermute(near, "remap", stay)
    by_c, rounds[1] = lax.optimization_barrier((by_c, rounds[1]))
    every = jnp.arange(blocks, dtype=jnp.int32)
    (sent,) = route(by_c, c_at, every, [(BINS, LEFT)], c_rows, True)
    (far,) = route(by_c, c_at, info[split:levels], in_bins, c_rows, False)
    (own,) = route(by_c, c_at, info[levels:blocks], in_bins, c_rows, False)
    left_at = own_left(BINS * IRREPS, LEFT * IRREPS)
    sent, left_at, near, rounds[2], code, irr_rows, sym_ab = lax.optimization_barrier(
        (sent, left_at, near, rounds[2], code, irr_rows, sym_ab)
    )
    other = [near, lax.ppermute(far, "remap", stay)]
    total = left_term(sent, left_rows(integrals, code, *left_at))
    rounds[-1], total = lax.optimization_barrier((rounds[-1], total))
    mine = 0
    for t, parts in enumerate(rounds):
        ways = [blocks + 2 * t, blocks + 2 * t + 1]
        if t == 0:
            ways, parts = ways[:1], parts[:1]
        reach = max(row[way] for row in plan for way in ways)
        if t == levels - 1:
            chosen = choose(ways, own, other, info, irr_rows)
            mine = last_product(ways, parts, mine, chosen, info, sym_ab[None, :])
            continue
        mine += bins_product(ways, parts, own, other[: 1 + (reach >= split)], info, irr_rows, sym_ab[None, :])

    def next_round(index, total):
        first = slots + index * more
        c_at = jnp.maximum(table(places, first, more) - 1, 0)
        (sent,) = route(by_c, c_at, every, [(0, LEFT_MORE)], c_rows, True)
        return total + left_term(sent, left_rows(integrals, code, *own_left(first, more)))

    total = lax.fori_loop(0, more_rounds, next_round, total)

    total = total.reshape(blocks, pair_rows, ab_cols)
    ids = jnp.arange(blocks)[:, None, None]
    total = total + jnp.where(ids == block, mine[None, :pair_rows], 0.0)
    total = total + jnp.where(ids == level * sides + 1 - side, mine[None, pair_rows:], 0.0)
    return reduce_to_owners(0.5 * total.reshape(blocks * pair_rows, ab_cols))


def solution(mesh):
    in_specs = (P("remap", None, "rep"), P("remap", "rep", None), P(), P())
    out_specs = P("remap", "rep")
    return jax.shard_map(body, mesh=mesh, in_specs=in_specs, out_specs=out_specs, check_vma=False)
```
